128 devices in a mesh: gz: 8 (over y, core), ta: 16 (over x, z).
Axes of the slice: x: 4, y: 4, z: 4, core: 2. Of those that a mesh axis runs over, the one named last changes fastest.
Arguments:
- basis: bfloat16 [2048, 128, 3072], P(('gz', 'ta')), may hold values from -0.078125 to 0.078125
- sources: bfloat16 [2048, 24, 3072], P(('gz', 'ta')), may hold values from -2000 to 2000
- old_coeffs: bfloat16 [32768, 3200], P(('gz', 'ta')), may hold values from -0.01171875 to 0.01171875
- eigenvalues: float32 [400], replicated, may hold values from 0.00239208 to 0.023920799
- dest_owner: int32 [32768], P(('gz', 'ta')), may hold values from 0 to 127, as said below
- new_pos: int32 [32768], P(('gz', 'ta')), may hold values from 0 to 255, as said below
Outputs:
- guesses: float32 [2048, 24, 3072], P(('gz', 'ta'))
- correlations: float32 [400, 24], replicated
The draws below stay inside these ranges and needn't reach their ends.
Inputs may be any that keep to these rules, and one draw needn't show every extreme that they name: `dest_owner`: on every device no owner is named by more than 4 records and some owner by exactly 4; over all devices every owner is named by exactly 256 records. `new_pos`: the records naming one owner carry distinct rows.
All inputs are finite; a program needn't handle non-finite values.
Results may differ from the reference program's by a relative error of at most 0.007.
Values may be sent and summed in bfloat16 or wider, within the bound.
A program may use at most 64 MiB of HBM per device.

```python
import math
import jax
import jax.numpy as jnp
from jax import lax

NB = 64
BV = 3072
MODES = 400
S = 12
BLK_DEV = 16
MG = 25
NBLK = 2048
RECS_DEV = 256
NREC = 32768
N_GZ = 8
N_TA = 16


def shuffled(subkey):
    return jax.random.permutation(subkey, RECS_DEV).astype(jnp.int32)


def route_tables(key):
    device_count = NREC // RECS_DEV
    half_count = device_count // 2
    share = RECS_DEV // device_count
    subkeys = jax.random.split(key, 6)
    pairing = jax.random.permutation(subkeys[0], device_count).astype(jnp.int32)
    spread = jax.random.randint(subkeys[1], (half_count,), 0, share + 1).astype(jnp.int32)
    spread = spread.at[0].set(share)
    counts = jnp.zeros((device_count,), jnp.int32)
    counts = counts.at[pairing[:half_count]].set(share + spread)
    counts = counts.at[pairing[half_count:]].set(share - spread)
    ends = jnp.cumsum(counts).astype(jnp.int32)
    slot_ids = jnp.arange(RECS_DEV, dtype=jnp.int32)
    section = jnp.sum((ends[None, :] <= slot_ids[:, None]).astype(jnp.int32), axis=1)
    offsets = jax.random.permutation(subkeys[2], device_count).astype(jnp.int32)
    labels = jax.random.permutation(subkeys[3], device_count).astype(jnp.int32)
    owner = labels[(offsets[:, None] + section[None, :]) % device_count]
    arrival = jax.vmap(shuffled)(jax.random.split(subkeys[4], device_count))
    position = arrival[owner, slot_ids[None, :]]
    storage = jax.vmap(shuffled)(jax.random.split(subkeys[5], device_count))
    owner = jnp.take_along_axis(owner, storage, axis=1)
    position = jnp.take_along_axis(position, storage, axis=1)
    return (owner.reshape(-1).astype(jnp.int32), position.reshape(-1).astype(jnp.int32))


def draw_dest_owner(key, part):
    return route_tables(key)[0]


def draw_new_pos(key, part):
    return route_tables(key)[1]


def draw_sources(key, part):
    key = jax.random.fold_in(key, 7)
    subkeys = jax.random.split(key, 4)
    block_ids = jnp.arange(NBLK)
    device_ids = block_ids // BLK_DEV
    slab_index = (device_ids // N_TA).astype(jnp.float32)
    time_index = (device_ids % N_TA).astype(jnp.float32)
    jitter = jax.random.uniform(subkeys[0], (NBLK, 2))
    exponent = 0.5 * (slab_index + jitter[:, 0]) / N_GZ + 0.5 * (time_index + jitter[:, 1]) / N_TA
    entries = jax.random.normal(subkeys[1], (NBLK, 2 * S, BV))
    row_scale = jnp.exp(math.log(10.0) * exponent)
    column_scale = jnp.exp(math.log(10.0) * jax.random.uniform(subkeys[3], (BV,)))
    return (entries * row_scale[:, None, None] * column_scale[None, None, :]).astype(jnp.bfloat16)


def block_scale(key, shape, shards, least, largest):
    level = 1.0
    for axis_at, parts in shards:
        steps = jax.random.uniform(jax.random.fold_in(jax.random.fold_in(key, 6), axis_at), (parts,), jnp.float32, least / len(shards), largest / len(shards))
        level = level * jnp.repeat(jnp.exp(steps), shape[axis_at] // parts).reshape((-1,) + (1,) * (len(shape) - 1 - axis_at))
    return level


def bell_draw(stream_key, dims, scale, reach, shards=(), kind=jnp.bfloat16):
    values = scale * jax.random.normal(stream_key, dims, jnp.float32)
    if shards:
        values = values * block_scale(stream_key, dims, shards, -0.22, 0.18)
    return jnp.clip(values, -reach, reach).astype(kind)


def setup_inputs(seed: int = 0) -> dict:
    arg_keys = jax.random.split(jax.random.key(seed), 7)
    basis = bell_draw(arg_keys[0], (NBLK, 2 * NB, BV), (2 * BV) ** -0.5, 0.078125, ((0, 128),))
    sources = draw_sources(jax.random.fold_in(arg_keys[6], 71), 0)
    old_coeffs = bell_draw(arg_keys[2], (NREC, MG * 2 * NB), (2 * NBLK * NB) ** -0.5, 0.01171875, ((0, 128),))
    eigenvalues = jnp.clip(jnp.exp(jax.random.uniform(arg_keys[3], (MODES,), jnp.float32, math.log(0.00239208), math.log(0.023920799))), 0.00239208, 0.023920799)
    dest_owner = draw_dest_owner(jax.random.fold_in(arg_keys[6], 71), 0)
    new_pos = draw_new_pos(jax.random.fold_in(arg_keys[6], 71), 0)
    return dict(basis=basis, sources=sources, old_coeffs=old_coeffs, eigenvalues=eigenvalues, dest_owner=dest_owner, new_pos=new_pos)


def reference(basis, sources, old_coeffs, eigenvalues, dest_owner, new_pos):
    rows_at = (dest_owner * RECS_DEV + new_pos).astype(jnp.int32)
    placed = jnp.zeros_like(old_coeffs).at[rows_at].set(old_coeffs)
    coeffs = placed.reshape(NBLK, MODES, 2 * NB)

    def project(block):
        vectors, field, coeff_table = block
        products = jnp.dot(vectors, field.T, preferred_element_type=jnp.float32)
        real_half = (products[:NB, :S] + products[NB:, S:]).astype(jnp.bfloat16)
        imag_half = (products[:NB, S:] - products[NB:, :S]).astype(jnp.bfloat16)
        stacked = jnp.concatenate([jnp.concatenate([real_half, imag_half], 1), jnp.concatenate([imag_half, -real_half], 1)], 0)
        term = jnp.dot(coeff_table, stacked, preferred_element_type=jnp.float32)
        widened = field.astype(jnp.float32)
        return (term, lax.optimization_barrier(jnp.sum(widened * widened, axis=1)))
    terms, squares = lax.map(project, (basis, sources, coeffs))
    proj = lax.optimization_barrier(jnp.sum(terms, axis=0))
    square_sum = lax.optimization_barrier(jnp.sum(squares, axis=0))
    norm_sq = square_sum[:S] + square_sum[S:]
    scale = jnp.sqrt(jnp.float32(2 * NBLK * BV)) * lax.rsqrt(norm_sq + 1e-06)
    correlations = proj * jnp.concatenate([scale, scale])[None, :]
    weights = (correlations / eigenvalues[:, None]).astype(jnp.bfloat16)

    def rebuild(block):
        vectors, coeff_table = block
        mixed = jnp.dot(coeff_table.T, weights, preferred_element_type=jnp.float32)
        real_coef = (mixed[:NB, :S] - mixed[NB:, S:]).astype(jnp.bfloat16)
        imag_coef = (mixed[:NB, S:] + mixed[NB:, :S]).astype(jnp.bfloat16)
        stacked = jnp.concatenate([jnp.concatenate([real_coef.T, -imag_coef.T], 1), jnp.concatenate([imag_coef.T, real_coef.T], 1)], 0)
        return jnp.dot(stacked, vectors, preferred_element_type=jnp.float32)
    guesses = lax.map(rebuild, (basis, coeffs))
    return (guesses, correlations)
```

```python
import functools

import jax
import jax.numpy as jnp
from jax import lax
from jax.experimental import pallas as pl
from jax.experimental.pallas import tpu as pltpu
from jax.sharding import PartitionSpec as P

F32 = jnp.float32
BF16 = jnp.bfloat16
MESH = pl.DeviceIdType.MESH

NB = 64
LN = 2 * NB
BV = 3072
S = 12
BLK = 16
MG = 25
MP = 32
GROUPS = 16
RECS = 256
MODES = 400
W = S * LN
PW = W // 3
SAME = 64 * BLK
MIB = 1 << 20


class Place:
    def __init__(self):
        gz = lax.axis_index("gz")
        ta = lax.axis_index("ta")
        self.core = lax.rem(gz, 2)
        self.c = (ta // 4, gz // 2, lax.rem(ta, 4))

    def at(self, axis, d):
        return lax.rem(self.c[axis] + d, 4)

    def device(self, axis, d):
        x, y, z = (self.at(a, d) if a == axis else self.c[a] for a in range(3))
        return (y * 2 + self.core, x * 4 + z)

    def sibling(self):
        x, y, z = self.c
        return (y * 2 + 1 - self.core, x * 4 + z)


def order(p):
    return (p % 3, (p + 1) % 3, (p + 2) % 3)


class Copies:
    def __init__(self, send, recv):
        self.send, self.recv, self.all = send, recv, []

    def start(self, src, dst, device):
        n = len(self.all)
        copy = pltpu.make_async_remote_copy(
            src_ref=src,
            dst_ref=dst,
            send_sem=self.send.at[n],
            recv_sem=self.recv.at[n],
            device_id=device,
            device_id_type=MESH,
        )
        copy.start()
        self.all.append(copy)
        return copy

    def finish(self):
        for copy in self.all:
            copy.wait_send()


def enter(devices):
    barrier = pltpu.get_barrier_semaphore()
    for device in devices:
        pl.semaphore_signal(barrier, inc=1, device_id=device, device_id_type=MESH)
    pl.semaphore_wait(barrier, len(devices))


def partners(place):
    return [place.sibling()] + [place.device(a, d) for a in range(3) for d in (1, 2, 3)]


def low_lanes(shape):
    return lax.broadcasted_iota(jnp.int32, shape, 1) % LN < NB


N_GATHER = 3 * (3 + 4 + 16) + 2 + 3


def gather_kernel(
    basis, sources, keys_col, keys_row, picked, squares, rows_both,
    bbuf, sbuf, prod, stage, table, cols, mine, theirs, got, bsem, ssem, send, recv,
):
    place = Place()
    core = place.core
    for b in range(BLK):
        pltpu.make_async_copy(sources.at[b], sbuf.at[b], ssem.at[b]).start()
        pltpu.make_async_copy(basis.at[b], bbuf.at[b], bsem.at[b]).start()
    enter(partners(place))
    copies = Copies(send, recv)
    cols[0] = keys_col[...]
    rows_both[0] = keys_row[...]
    sib = place.sibling()
    key_copies = [
        copies.start(cols.at[0], cols.at[1], sib),
        copies.start(rows_both.at[0], rows_both.at[1], sib),
    ]

    def block(b, total):
        pltpu.make_async_copy(sources.at[b], sbuf.at[b], ssem.at[b]).wait()
        pltpu.make_async_copy(basis.at[b], bbuf.at[b], bsem.at[b]).wait()
        field = sbuf[b]
        prod[...] = lax.dot_general(
            field, bbuf[b], (((1,), (1,)), ((), ())), preferred_element_type=F32
        )
        a = prod[0:S, :]
        other = pltpu.roll(prod[S : 2 * S, :], NB, 1)
        stage[pl.ds(pl.multiple_of(b * 16, 16), S), :] = other + jnp.where(low_lanes((S, LN)), a, -a)
        wide = field.astype(F32)
        wide = wide * wide
        for t in range(BV // LN):
            total = total + wide[:, t * LN : (t + 1) * LN]
        return total

    squares[...] = lax.fori_loop(0, BLK, block, jnp.zeros((2 * S, LN), F32))

    def row(c3, c2, c1=0):
        return pl.multiple_of(((c3 * 4 + c2) * 4 + c1) * BLK, BLK)

    def rows(p, start, size):
        return table.at[p, pl.ds(start, size), :]

    first = []
    for p in range(3):
        a1, a2, a3 = order(p)
        here = row(place.c[a3], place.c[a2], place.c[a1])
        part = [stage[pl.ds(s, BLK, stride=16), :] for s in range(p * 4, p * 4 + 4)]
        table[p, pl.ds(here, BLK), :] = jnp.concatenate(part, axis=1).astype(BF16)
        first.append(
            [copies.start(rows(p, here, BLK), rows(p, here, BLK), place.device(a1, d)) for d in (1, 3, 2)]
        )

    def both(p, axis, start, size):
        ref = rows(p, start, size)
        return [copies.start(ref, ref, place.device(axis, d)) for d in (1, 3)]

    def forward(p, axis, left, right, size):
        half = size // 2
        a = rows(p, left, half)
        b = rows(p, pl.multiple_of(right + half, BLK), half)
        return [
            copies.start(a, a, place.device(axis, 1)),
            copies.start(b, b, place.device(axis, 3)),
        ]

    def arrived(pair):
        for copy in pair:
            copy.wait_recv()

    line = 4 * BLK
    second, third = [], [[], [], []]
    for p in range(3):
        _, a2, a3 = order(p)
        arrived(first[p])
        start = row(place.c[a3], place.c[a2])
        second.append(both(p, a2, start, line))
        third[p].append(both(p, a3, start, line))
    halves = []
    for p in range(3):
        _, a2, a3 = order(p)
        c3 = place.c[a3]
        arrived(second[p])
        left, right = row(c3, place.at(a2, 3)), row(c3, place.at(a2, 1))
        halves.append(forward(p, a2, left, right, line))
        third[p].append(both(p, a3, left, line))
        third[p].append(both(p, a3, right, line))
    for p in range(3):
        _, a2, a3 = order(p)
        arrived(halves[p])
        third[p].append(both(p, a3, row(place.c[a3], place.at(a2, 2)), line))
    last = [[], [], []]
    for j, d in enumerate((0, 3, 1, 2)):
        for p in range(3):
            _, a2, a3 = order(p)
            c2 = place.at(a2, d)
            arrived(third[p][j])
            last[p].append(
                forward(p, a3, row(place.at(a3, 3), c2), row(place.at(a3, 1), c2), line)
            )
    arrived(key_copies)
    sent = []
    for p in range(3):
        for pair in last[p]:
            arrived(pair)
        lanes = slice(p * PW, (p + 1) * PW)
        ids = lax.broadcasted_iota(jnp.int32, (RECS, SAME), 1) + core * SAME
        for who, out in ((1, theirs), (0, mine)):
            key = cols[who, :, p : p + 1]
            pick = jnp.where(key == ids, 1.0, 0.0).astype(BF16)
            out[p] = jnp.dot(pick, table[p], preferred_element_type=F32).astype(BF16)
            if who == 1:
                sent.append(copies.start(theirs.at[p], got.at[p], sib))
    for p in range(3):
        sent[p].wait_recv()
        picked[:, p * PW : (p + 1) * PW] = mine[p] + got[p]
    copies.finish()


def gather_projections(basis, sources, keys_col, keys_row):
    any_space = pl.BlockSpec(memory_space=pl.ANY)
    vmem = pl.BlockSpec(memory_space=pltpu.VMEM)
    return pl.pallas_call(
        gather_kernel,
        out_shape=(
            jax.ShapeDtypeStruct((RECS, W), BF16),
            jax.ShapeDtypeStruct((2 * S, LN), F32),
            jax.ShapeDtypeStruct((2, 8, RECS), jnp.int32),
        ),
        in_specs=[any_space, any_space, vmem, vmem],
        out_specs=(vmem, vmem, vmem),
        scratch_shapes=[
            pltpu.VMEM((BLK, LN, BV), BF16),
            pltpu.VMEM((BLK, 2 * S, BV), BF16),
            pltpu.VMEM((2 * S, LN), F32),
            pltpu.VMEM((BLK * 16, LN), F32),
            pltpu.VMEM((3, SAME, PW), BF16),
            pltpu.VMEM((2, RECS, LN), jnp.int32),
            pltpu.VMEM((3, RECS, PW), BF16),
            pltpu.VMEM((3, RECS, PW), BF16),
            pltpu.VMEM((3, RECS, PW), BF16),
            pltpu.SemaphoreType.DMA((BLK,)),
            pltpu.SemaphoreType.DMA((BLK,)),
            pltpu.SemaphoreType.DMA((N_GATHER,)),
            pltpu.SemaphoreType.DMA((N_GATHER,)),
        ],
        compiler_params=pltpu.CompilerParams(
            collective_id=1, has_side_effects=True, vmem_limit_bytes=48 * MIB
        ),
    )(basis, sources, keys_col, keys_row)


def spread_records(coeffs, spread):
    for m in range(MG):
        spread[pl.ds(m, RECS, stride=MP), :] = coeffs[:, m * LN : (m + 1) * LN].astype(F32)
    for m in range(MG, MP):
        spread[pl.ds(m, RECS, stride=MP), :] = jnp.zeros((RECS, LN), F32)


def project_kernel(group, coeffs, picked, out, spread, tall, acc):
    spread_records(coeffs, spread)
    for s in range(S):
        tall[pl.ds(s, RECS, stride=16), :] = picked[:, s * LN : (s + 1) * LN].astype(F32)
    for s in range(S, 16):
        tall[pl.ds(s, RECS, stride=16), :] = jnp.zeros((RECS, LN), F32)
    acc[...] = jnp.zeros_like(acc)
    low = low_lanes((16, LN))

    def record(i, carry):
        real = tall[pl.ds(pl.multiple_of(i * 16, 16), 16), :]
        turned = pltpu.roll(real, NB, 1)
        both = jnp.concatenate([real, jnp.where(low, turned, -turned)], axis=0).astype(BF16)
        modes = spread[pl.ds(pl.multiple_of(i * MP, MP), MP), :].astype(BF16)
        term = lax.dot_general(both, modes, (((1,), (1,)), ((), ())), preferred_element_type=F32)
        r = group[i]
        acc[r, :, 0:MP] += term
        return carry

    lax.fori_loop(0, RECS, record, 0, unroll=8)
    for q in range(4):
        total = acc[4 * q]
        for k in range(1, 4):
            total = total + pltpu.roll(acc[4 * q + k], k * MP, 1)
        out[:, q * LN : (q + 1) * LN] = total


def project_records(group, coeffs, picked):
    vmem = pl.BlockSpec(memory_space=pltpu.VMEM)
    return pl.pallas_call(
        project_kernel,
        out_shape=jax.ShapeDtypeStruct((2 * 16, GROUPS * MP), F32),
        in_specs=[pl.BlockSpec(memory_space=pltpu.SMEM), vmem, vmem],
        out_specs=vmem,
        scratch_shapes=[
            pltpu.VMEM((RECS * MP, LN), F32),
            pltpu.VMEM((RECS * 16, LN), F32),
            pltpu.VMEM((GROUPS, 32, LN), F32),
        ],
        compiler_params=pltpu.CompilerParams(vmem_limit_bytes=32 * MIB),
    )(group, coeffs, picked)


def mix_kernel(group, coeffs, weights, out, spread, wt, tall):
    spread_records(coeffs, spread)
    for r in range(GROUPS):
        tile = weights[:, (r // 4) * LN : (r // 4 + 1) * LN]
        wt[r] = tile if r % 4 == 0 else pltpu.roll(tile, LN - (r % 4) * MP, 1)
    low = low_lanes((16, LN))

    def record(i, carry):
        modes = spread[pl.ds(pl.multiple_of(i * MP, MP), MP), :].astype(BF16)
        r = group[i]
        w = wt[r][:, 0:MP].astype(BF16)
        mixed = jnp.dot(w, modes, preferred_element_type=F32)
        turned = pltpu.roll(mixed[16:32, :], NB, 1)
        tall[pl.ds(pl.multiple_of(i * 16, 16), 16), :] = mixed[0:16, :] + jnp.where(low, -turned, turned)
        return carry

    lax.fori_loop(0, RECS, record, 0, unroll=8)
    for s in range(S):
        out[:, s * LN : (s + 1) * LN] = tall[pl.ds(s, RECS, stride=16), :].astype(BF16)


def mix_records(group, coeffs, weights):
    vmem = pl.BlockSpec(memory_space=pltpu.VMEM)
    return pl.pallas_call(
        mix_kernel,
        out_shape=jax.ShapeDtypeStruct((RECS, W), BF16),
        in_specs=[pl.BlockSpec(memory_space=pltpu.SMEM), vmem, vmem],
        out_specs=vmem,
        scratch_shapes=[
            pltpu.VMEM((RECS * MP, LN), F32),
            pltpu.VMEM((GROUPS, 32, LN), F32),
            pltpu.VMEM((RECS * 16, LN), F32),
        ],
        compiler_params=pltpu.CompilerParams(vmem_limit_bytes=32 * MIB),
    )(group, coeffs, weights)


N_SUM = 2 + 27
CUTS = ((0, 8), (8, 16), (24, 8))


def sum_kernel(part, out, half_in, slots, whole, send, recv):
    place = Place()
    sib = place.sibling()
    enter(partners(place))
    copies = Copies(send, recv)
    width = GROUPS * MP // 2
    lanes = pl.ds(pl.multiple_of(place.core * width, width), width)
    other = pl.ds(pl.multiple_of((1 - place.core) * width, width), width)
    copies.start(part.at[:, other], half_in, sib).wait_recv()
    total = part[:, lanes] + half_in[...]
    pieces = [total[a : a + n] for a, n in CUTS]
    for step in range(3):
        waiting = []
        for p, (a, n) in enumerate(CUTS):
            axis = (p + step) % 3
            mine = place.c[axis]
            slots[step, mine, a : a + n, :] = pieces[p]
            ref = slots.at[step, mine, a : a + n, :]
            waiting.append([copies.start(ref, ref, place.device(axis, d)) for d in (1, 3, 2)])
        for p, (a, n) in enumerate(CUTS):
            for copy in waiting[p]:
                copy.wait_recv()
            got = [slots[step, c, a : a + n, :] for c in range(4)]
            pieces[p] = (got[0] + got[1]) + (got[2] + got[3])
    for p, (a, n) in enumerate(CUTS):
        whole[a : a + n, lanes] = pieces[p]
    ref = whole.at[:, lanes]
    copies.start(ref, ref, sib).wait_recv()
    out[...] = whole[...]
    copies.finish()


def sum_everywhere(part):
    vmem = pl.BlockSpec(memory_space=pltpu.VMEM)
    return pl.pallas_call(
        sum_kernel,
        out_shape=jax.ShapeDtypeStruct(part.shape, F32),
        in_specs=[vmem],
        out_specs=vmem,
        scratch_shapes=[
            pltpu.VMEM((32, GROUPS * MP // 2), F32),
            pltpu.VMEM((3, 4, 32, GROUPS * MP // 2), F32),
            pltpu.VMEM((32, GROUPS * MP), F32),
            pltpu.SemaphoreType.DMA((N_SUM,)),
            pltpu.SemaphoreType.DMA((N_SUM,)),
        ],
        compiler_params=pltpu.CompilerParams(collective_id=2, has_side_effects=True),
    )(part)


N_REDUCE = 1 + 3 * (4 + 4 + 3)


def reduce_kernel(
    mixed, keys, out, both, x, far_out, far_in, near_out, near_in,
    far2_out, far2_in, near2_out, near2_in, own_out, own_in, send, recv,
):
    place = Place()
    core = place.core
    sib = place.sibling()
    enter(partners(place))
    copies = Copies(send, recv)
    both[0] = mixed[...]
    exchange = copies.start(both.at[0], both.at[1], sib)
    exchange.wait_recv()
    plane, line = 16 * BLK, 4 * BLK

    def partial(p, c3):
        base = core * SAME + c3 * plane
        ids = lax.broadcasted_iota(jnp.int32, (plane, RECS), 0) + base
        total = None
        for who in range(2):
            pick = jnp.where(keys[who, p : p + 1, :] == ids, 1.0, 0.0).astype(BF16)
            term = jnp.dot(pick, both[who, :, p * PW : (p + 1) * PW], preferred_element_type=F32)
            total = term if total is None else total + term
        return total

    far = []
    for p in range(3):
        a3 = order(p)[2]
        far_out[p] = partial(p, place.at(a3, 2)).astype(BF16)
        half = plane // 2
        far.append([
            copies.start(far_out.at[p, 0:half, :], far_in.at[p, 0], place.device(a3, 1)),
            copies.start(far_out.at[p, half:plane, :], far_in.at[p, 1], place.device(a3, 3)),
        ])
    near = []
    for p in range(3):
        a3 = order(p)[2]
        half = plane // 2
        pair = []
        for k, d in enumerate((1, 3)):
            total = partial(p, place.at(a3, d))
            far[p][k].wait_recv()
            more = far_in[p, k].astype(F32)
            if k == 0:
                near_out[p, k, 0:half, :] = (total[0:half] + more).astype(BF16)
                near_out[p, k, half:plane, :] = total[half:plane].astype(BF16)
            else:
                near_out[p, k, 0:half, :] = total[0:half].astype(BF16)
                near_out[p, k, half:plane, :] = (total[half:plane] + more).astype(BF16)
            pair.append(copies.start(near_out.at[p, k], near_in.at[p, k], place.device(a3, d)))
        near.append(pair)
    for p in range(3):
        x[p] = partial(p, place.c[order(p)[2]])
    far2 = []
    for p in range(3):
        a2 = order(p)[1]
        near[p][0].wait_recv()
        near[p][1].wait_recv()
        x[p] = x[p] + near_in[p, 0].astype(F32) + near_in[p, 1].astype(F32)
        c = pl.multiple_of(place.at(a2, 2) * line, line)
        half = line // 2
        far2_out[p] = x[p, pl.ds(c, line), :].astype(BF16)
        far2.append([
            copies.start(far2_out.at[p, 0:half, :], far2_in.at[p, 0], place.device(a2, 1)),
            copies.start(far2_out.at[p, half:line, :], far2_in.at[p, 1], place.device(a2, 3)),
        ])
    near2 = []
    for p in range(3):
        a2 = order(p)[1]
        half = line // 2
        pair = []
        for k, d in enumerate((1, 3)):
            far2[p][k].wait_recv()
            total = x[p, pl.ds(pl.multiple_of(place.at(a2, d) * line, line), line), :]
            more = far2_in[p, k].astype(F32)
            if k == 0:
                near2_out[p, k, 0:half, :] = (total[0:half] + more).astype(BF16)
                near2_out[p, k, half:line, :] = total[half:line].astype(BF16)
            else:
                near2_out[p, k, 0:half, :] = total[0:half].astype(BF16)
                near2_out[p, k, half:line, :] = (total[half:line] + more).astype(BF16)
            pair.append(copies.start(near2_out.at[p, k], near2_in.at[p, k], place.device(a2, d)))
        near2.append(pair)
    last = []
    for p in range(3):
        a1, a2, _ = order(p)
        near2[p][0].wait_recv()
        near2[p][1].wait_recv()
        total = x[p, pl.ds(pl.multiple_of(place.c[a2] * line, line), line), :]
        total = total + near2_in[p, 0].astype(F32) + near2_in[p, 1].astype(F32)
        x[p, 0:line, :] = total
        trio = []
        for k, d in enumerate((1, 3, 2)):
            c = pl.multiple_of(place.at(a1, d) * BLK, BLK)
            own_out[p, k] = x[p, pl.ds(c, BLK), :].astype(BF16)
            trio.append(copies.start(own_out.at[p, k], own_in.at[p, k], place.device(a1, d)))
        last.append(trio)
    for p in range(3):
        a1 = order(p)[0]
        total = x[p, pl.ds(pl.multiple_of(place.c[a1] * BLK, BLK), BLK), :]
        for k in range(3):
            last[p][k].wait_recv()
            total = total + own_in[p, k].astype(F32)
        out[:, p * PW : (p + 1) * PW] = total
    copies.finish()


def reduce_to_owners(mixed, keys):
    vmem = pl.BlockSpec(memory_space=pltpu.VMEM)
    plane, line = 16 * BLK, 4 * BLK
    return pl.pallas_call(
        reduce_kernel,
        out_shape=jax.ShapeDtypeStruct((BLK, W), F32),
        in_specs=[vmem, vmem],
        out_specs=vmem,
        scratch_shapes=[
            pltpu.VMEM((2, RECS, W), BF16),
            pltpu.VMEM((3, plane, PW), F32),
            pltpu.VMEM((3, plane, PW), BF16),
            pltpu.VMEM((3, 2, plane // 2, PW), BF16),
            pltpu.VMEM((3, 2, plane, PW), BF16),
            pltpu.VMEM((3, 2, plane, PW), BF16),
            pltpu.VMEM((3, line, PW), BF16),
            pltpu.VMEM((3, 2, line // 2, PW), BF16),
            pltpu.VMEM((3, 2, line, PW), BF16),
            pltpu.VMEM((3, 2, line, PW), BF16),
            pltpu.VMEM((3, 3, BLK, PW), BF16),
            pltpu.VMEM((3, 3, BLK, PW), BF16),
            pltpu.SemaphoreType.DMA((N_REDUCE,)),
            pltpu.SemaphoreType.DMA((N_REDUCE,)),
        ],
        compiler_params=pltpu.CompilerParams(
            collective_id=3, has_side_effects=True, vmem_limit_bytes=32 * MIB
        ),
    )(mixed, keys)


def guess_kernel(g, basis, out, tall, comb):
    b = pl.program_id(0)

    @pl.when(b == 0)
    def _():
        for s in range(S):
            tall[pl.ds(s, BLK, stride=16), :] = g[:, s * LN : (s + 1) * LN]

    mine = tall[pl.ds(pl.multiple_of(b * 16, 16), S), :]
    comb[0:S, :] = jnp.where(low_lanes((S, LN)), mine, -mine)
    comb[S : 2 * S, :] = pltpu.roll(mine, NB, 1)
    out[...] = jnp.dot(comb[...].astype(BF16), basis[0], preferred_element_type=F32)[None]


def make_guesses(g, basis):
    return pl.pallas_call(
        guess_kernel,
        out_shape=jax.ShapeDtypeStruct((BLK, 2 * S, BV), F32),
        grid=(BLK,),
        in_specs=[
            pl.BlockSpec((BLK, W), lambda b: (0, 0)),
            pl.BlockSpec((1, LN, BV), lambda b: (b, 0, 0)),
        ],
        out_specs=pl.BlockSpec((1, 2 * S, BV), lambda b: (b, 0, 0)),
        scratch_shapes=[
            pltpu.VMEM((BLK * 16, LN), F32),
            pltpu.VMEM((2 * S, LN), F32),
        ],
        compiler_params=pltpu.CompilerParams(vmem_limit_bytes=32 * MIB),
    )(g, basis)


def keys_of(dest_owner, new_pos):
    core = (dest_owner // 16) % 2
    c = ((dest_owner // 4) % 4, dest_owner // 32, dest_owner % 4)
    found = []
    for p in range(3):
        a1, a2, a3 = order(p)
        slot = ((core * 4 + c[a3]) * 4 + c[a2]) * 4 + c[a1]
        found.append(slot * BLK + new_pos // GROUPS)
    return jnp.stack(found)


def shards(basis, sources, old_coeffs, eigenvalues, dest_owner, new_pos):
    keys = keys_of(dest_owner, new_pos)
    group = new_pos % GROUPS
    keys_row = jnp.pad(keys, ((0, 5), (0, 0)))
    keys_col = jnp.pad(keys.T, ((0, 0), (0, LN - 3)))
    picked, squares, rows_both = gather_projections(basis, sources, keys_col, keys_row)
    part = project_records(group, old_coeffs, picked)
    local = jnp.sum(squares, axis=1)
    local = jnp.pad(local[:S] + local[S:], (0, 4))
    part = part.at[:, MG].set(jnp.concatenate([local, local]))
    total = sum_everywhere(part)
    norm_sq = total[:, MG]
    scale = jnp.sqrt(jnp.float32(2 * 128 * BLK * BV)) * lax.rsqrt(norm_sq + 1e-06)
    scaled = (total * scale[:, None]).reshape(32, GROUPS, MP)[:, :, :MG]
    correlations = jnp.concatenate([scaled[0:S], scaled[16 : 16 + S]]).reshape(2 * S, MODES).T
    weights = (scaled / eigenvalues.reshape(1, GROUPS, MG)).astype(BF16).astype(F32)
    weights = jnp.pad(weights, ((0, 0), (0, 0), (0, MP - MG))).reshape(32, GROUPS * MP)
    mixed = mix_records(group, old_coeffs, weights)
    g = reduce_to_owners(mixed, rows_both)
    return make_guesses(g, basis), correlations


def solution(mesh):
    in_specs = (
        P(("gz", "ta"), None, None),
        P(("gz", "ta"), None, None),
        P(("gz", "ta"), None),
        P(),
        P(("gz", "ta")),
        P(("gz", "ta")),
    )
    out_specs = (P(("gz", "ta"), None, None), P())
    return jax.shard_map(shards, mesh=mesh, in_specs=in_specs, out_specs=out_specs, check_vma=False)
```

```python
import jax
import jax.numpy as jnp
from jax import lax
from jax.experimental import pallas as pl
from jax.experimental.pallas import tpu as pltpu
from jax.sharding import PartitionSpec as P

F32 = jnp.float32
BF16 = jnp.bfloat16
I32 = jnp.int32
MESH = pl.DeviceIdType.MESH

NB = 64
LN = 2 * NB
BV = 3072
S = 12
BLK = 16
MG = 25
MP = 32
GROUPS = 16
RECS = 256
MODES = 400
H = 2
SH = S // H
PARTS = 3 * H
PW = 2 * LN
HW = SH * LN
RR = 16
SAME = 64 * BLK
PLANE, LINE = 16 * BLK, 4 * BLK
MIB = 1 << 20
N_COPIES = 1 + PARTS * 22 + PARTS + H * (14 + 6 + 14) + H + PARTS * 10


class Place:
    def __init__(self):
        gz = lax.axis_index("gz")
        ta = lax.axis_index("ta")
        self.core = lax.rem(gz, 2)
        self.c = (ta // 4, gz // 2, lax.rem(ta, 4))

    def at(self, axis, d):
        return lax.rem(self.c[axis] + d, 4)

    def device(self, axis, d, flip=False):
        x, y, z = (self.at(a, d) if a == axis else self.c[a] for a in range(3))
        return (y * 2 + (1 - self.core if flip else self.core), x * 4 + z)


def order(q):
    return (q % 3, (q + 1) % 3, (q + 2) % 3)


class Copies:
    def __init__(self, send, recv):
        self.send, self.recv, self.all = send, recv, []

    def start(self, src, dst, device):
        n = len(self.all)
        copy = pltpu.make_async_remote_copy(
            src_ref=src,
            dst_ref=dst,
            send_sem=self.send.at[n],
            recv_sem=self.recv.at[n],
            device_id=device,
            device_id_type=MESH,
        )
        copy.start()
        self.all.append(copy)
        return copy

    def finish(self):
        for copy in self.all:
            copy.wait_send()


def arrived(copies):
    for copy in copies:
        copy.wait_recv()


def iota(shape, axis):
    return lax.broadcasted_iota(I32, shape, axis)


def low_lanes(shape):
    return iota(shape, 1) % LN < NB


def spread_lanes(x):
    x = x + pltpu.roll(x, 2 * MP, 1)
    return x + pltpu.roll(x, MP, 1)


def kernel(
    basis, sources, coeffs_in, owner_in, pos_in, pos, eig_in,
    guesses, corr_out,
    bbuf, sbuf, prod, stage, sq, table, idsb, lane_group, eig, terms, coeffs, kbig, kcol, pick, pick_t, wide, modes,
    mine, theirs, got, xs, pay, ar1, ar2, ar3, corr, wt, tall, both,
    far_out, far_in, near_out, near_in, x, line_out, line_in, own_out, own_in, gs, comb, gout,
    bsem, ssem, osem, csem, send, recv,
):
    place = Place()
    core = place.core
    sib = place.device(0, 0, True)
    copies = Copies(send, recv)

    def pair_load(j):
        at = pl.ds(j * 2, 2)
        return (
            pltpu.make_async_copy(sources.at[at], sbuf.at[at], ssem.at[j]),
            pltpu.make_async_copy(basis.at[at], bbuf.at[at], bsem.at[j]),
        )

    for j in range(3):
        for copy in pair_load(j):
            copy.start()
    load_coeffs = pltpu.make_async_copy(coeffs_in, coeffs, csem)
    load_coeffs.start()
    barrier = pltpu.get_barrier_semaphore()
    friends = [sib] + [place.device(a, d, f) for a in range(3) for d in (1, 2, 3) for f in (False, True)]
    for friend in friends:
        pl.semaphore_signal(barrier, inc=1, device_id=friend, device_id_type=MESH)

    low12 = low_lanes((S, LN))

    def block_pair(j, total):
        for copy in pair_load(j):
            copy.wait()

        @pl.when(j + 3 < BLK // 2)
        def _():
            for copy in pair_load(j + 3):
                copy.start()

        at = pl.ds(j * 2, 2)
        field = sbuf[at].reshape(4 * S, BV)
        vectors = bbuf[at].reshape(2 * LN, BV)
        prod[...] = lax.dot_general(
            field, vectors, (((1,), (1,)), ((), ())), preferred_element_type=F32
        )
        for k in range(2):
            lanes = slice(k * LN, (k + 1) * LN)
            a = prod[2 * S * k : 2 * S * k + S, lanes]
            b = pltpu.roll(prod[2 * S * k + S : 2 * S * k + 2 * S, lanes], NB, 1)
            stage[pl.ds(pl.multiple_of((j * 2 + k) * 16, 16), S), :] = b + jnp.where(low12, a, -a)
        wide_field = field.astype(F32)
        wide_field = wide_field * wide_field
        for t in range(BV // LN):
            total = total + wide_field[:, t * LN : (t + 1) * LN]
        return total

    total = lax.fori_loop(0, BLK // 2, block_pair, jnp.zeros((4 * S, LN), F32))
    sq[...] = jnp.broadcast_to(
        jnp.sum(total[0 : 2 * S] + total[2 * S : 4 * S], axis=1, keepdims=True), (2 * S, LN)
    )
    pl.semaphore_wait(barrier, len(friends))

    def row(c3, c2, c1=0):
        return pl.multiple_of(((c3 * 4 + c2) * 4 + c1) * BLK, BLK)

    def rows(q, start, size):
        return table.at[q, pl.ds(start, size), :]

    first, second, third, last = {}, {}, {}, {}

    def to_axis(q, axis, start, size, ds):
        ref = rows(q, start, size)
        return [copies.start(ref, ref, place.device(axis, d)) for d in ds]

    def ag1(q):
        a1, a2, a3 = order(q)
        here = row(place.c[a3], place.c[a2], place.c[a1])
        s = q * 2
        own = [stage[pl.ds(s + k, BLK, stride=16), :] for k in range(2)]
        table[q, pl.ds(here, BLK), :] = jnp.concatenate(own, axis=1).astype(BF16)
        first[q] = to_axis(q, a1, here, BLK, (1, 3, 2))

    def ag2(q):
        _, a2, a3 = order(q)
        arrived(first[q])
        second[q] = to_axis(q, a2, row(place.c[a3], place.c[a2]), LINE, (1, 3, 2))

    def ag3(q, d):
        _, a2, a3 = order(q)
        if d:
            second[q][{3: 0, 1: 1, 2: 2}[d]].wait_recv()
        third[q, d] = to_axis(q, a3, row(place.c[a3], place.at(a2, d)), LINE, (1, 3))

    def ag_forward(q, d):
        _, a2, a3 = order(q)
        arrived(third[q, d])
        c2 = place.at(a2, d)
        half = LINE // 2
        a = rows(q, row(place.at(a3, 3), c2), half)
        b = rows(q, pl.multiple_of(row(place.at(a3, 1), c2) + half, BLK), half)
        last[q, d] = [
            copies.start(a, a, place.device(a3, 1)),
            copies.start(b, b, place.device(a3, 3)),
        ]

    def make_keys():
        kbig[...] = jnp.zeros_like(kbig)
        for who in range(2):
            owner, at = idsb[who, 0:1, :], idsb[who, 1:2, :]
            c = ((owner >> 2) & 3, owner >> 5, owner & 3)
            same = ((owner >> 4) & 1) == core
            for p in range(3):
                a1, a2, a3 = order(p)
                key = ((c[a3] * 4 + c[a2]) * 4 + c[a1]) * BLK + (at >> 4)
                key = jnp.where(same, key, -1)
                kbig[who * 3 + p : who * 3 + p + 1, :] = key.astype(F32)
        kcol[...] = kbig[...].T

    def make_picks():
        wide_ids = iota((RECS, SAME), 1).astype(F32)
        for who in range(2):
            for p in range(3):
                k = who * 3 + p
                pick[p, who] = jnp.where(kcol[:, k : k + 1] == wide_ids, 1.0, 0.0).astype(BF16)

    def make_picks_t():
        tall_ids = iota((SAME, RECS), 0).astype(F32)
        for who in range(2):
            for p in range(3):
                k = who * 3 + p
                pick_t[p, :, who * RECS : (who + 1) * RECS] = jnp.where(
                    kbig[k : k + 1, :] == tall_ids, 1.0, 0.0
                ).astype(BF16)

    def make_modes():
        for m in range(MG):
            wide[pl.ds(m, RECS, stride=MP), :] = coeffs[:, m * LN : (m + 1) * LN].astype(F32)
        for m in range(MG, MP):
            wide[pl.ds(m, RECS, stride=MP), :] = jnp.zeros((RECS, LN), F32)
        modes[...] = wide[...].astype(BF16)

    def make_tables():
        i = iota((RECS // 4, RECS), 1)
        group = jnp.where(i // 4 == iota((RECS // 4, RECS), 0), pos_in[...] & (GROUPS - 1), 0)
        lanes = iota((RECS, LN), 0) % 4 == iota((RECS, LN), 1) // MP
        lane_group[...] = jnp.dot(
            group.astype(F32).astype(BF16),
            jnp.where(lanes, 1.0, 0.0).astype(BF16),
            preferred_element_type=F32,
        )
        wide_eig = jnp.concatenate([eig_in[...], jnp.ones((1, GROUPS * MP - MODES), F32)], axis=1)
        lane = iota((1, GROUPS * MP), 1)
        padded = jnp.full((1, GROUPS * MP), jnp.inf, F32)
        for r in range(GROUPS):
            moved = pltpu.roll(wide_eig, r * (MP - MG), 1) if r else wide_eig
            padded = jnp.where((lane // MP == r) & (lane % MP < MG), moved, padded)
        eig[...] = jnp.broadcast_to(padded, eig.shape)

    exchange = {}

    def gather(h):
        for p in range(3):
            q = h * 3 + p
            for d in range(4):
                arrived(last[q, d])
            theirs[q] = jnp.dot(pick[p, 1], table[q], preferred_element_type=F32).astype(BF16)
            exchange[q] = copies.start(theirs.at[q], got.at[q], sib)
        for p in range(3):
            q = h * 3 + p
            mine[q] = jnp.dot(pick[p, 0], table[q], preferred_element_type=F32).astype(BF16)

    low_rec = low_lanes((RECS, LN))
    group32 = iota((RR, LN), 1) // MP

    def project(h):
        for s in (6, 7, 14, 15):
            xs[pl.ds(s, RECS, stride=RR), :] = jnp.zeros((RECS, LN), F32)
        for p in range(3):
            q = h * 3 + p
            exchange[q].wait_recv()
            both_cores = mine[q].astype(F32) + got[q].astype(F32)
            for k in range(2):
                real = both_cores[:, k * LN : (k + 1) * LN]
                turned = pltpu.roll(real, NB, 1)
                xs[pl.ds(2 * p + k, RECS, stride=RR), :] = real
                xs[pl.ds(8 + 2 * p + k, RECS, stride=RR), :] = jnp.where(low_rec, turned, -turned)

        def eight(g, carry):
            left = xs[pl.ds(pl.multiple_of(g * 8 * RR, 8 * RR), 8 * RR), :].astype(BF16)
            right = modes[pl.ds(pl.multiple_of(g * 8 * MP, 8 * MP), 8 * MP), :]
            out = lax.dot_general(left, right, (((1,), (1,)), ((), ())), preferred_element_type=F32)
            for t in range(2):
                lanes = slice(t * LN, (t + 1) * LN)
                term = out[4 * t * RR : (4 * t + 1) * RR, lanes]
                for k in range(1, 4):
                    a = 4 * t + k
                    term = jnp.where(group32 == k, out[a * RR : (a + 1) * RR, lanes], term)
                terms[pl.ds(pl.multiple_of((g * 2 + t) * RR, RR), RR), :] = term
            return carry

        lax.fori_loop(0, RECS // 8, eight, 0, unroll=4)

        def four(g, acc):
            term = terms[pl.ds(pl.multiple_of(g * RR, RR), RR), :]
            whose = lane_group[pl.ds(g, 1), :]
            return tuple(acc[r] + jnp.where(whose == float(r), term, 0.0) for r in range(GROUPS))

        acc = lax.fori_loop(0, RECS // 4, four, (jnp.zeros((RR, LN), F32),) * GROUPS, unroll=4)
        for t in range(4):
            tile = spread_lanes(acc[4 * t])
            for k in range(1, 4):
                tile = jnp.where(group32 == k, spread_lanes(acc[4 * t + k]), tile)
            pay[h, :, t * LN : (t + 1) * LN] = tile
        norm = sq[h * SH : (h + 1) * SH, :] + sq[S + h * SH : S + (h + 1) * SH, :]
        lane = iota((SH, LN), 1)
        for base in (0, 8):
            old = pay[h, base : base + SH, 0:LN]
            pay[h, base : base + SH, 0:LN] = jnp.where(lane == MG, norm, old)

    steps = {}
    half_lanes = GROUPS * MP // 2

    def axis_of(h, v, step):
        return (v + h + step) % 3

    def sum1(h):
        for v in range(2):
            axis = axis_of(h, v, 0)
            slot = place.c[axis] * 2 + core
            piece = slice(8 * v, 8 * v + 8)
            ours = pl.ds(pl.multiple_of(core * half_lanes, half_lanes), half_lanes)
            other = pl.ds(pl.multiple_of((1 - core) * half_lanes, half_lanes), half_lanes)
            ar1[h, v, slot] = pay[h, piece, ours]
            dst = ar1.at[h, v, slot]
            steps[1, h, v] = [
                copies.start(pay.at[h, piece, other if f else ours], dst, place.device(axis, d, f))
                for d in (0, 1, 3, 2) for f in (False, True) if d or f
            ]

    def sum2(h):
        for v in range(2):
            arrived(steps[1, h, v])
            total = ar1[h, v, 0]
            for k in range(1, 8):
                total = total + ar1[h, v, k]
            axis = axis_of(h, v, 1)
            slot = place.c[axis]
            ar2[h, v, slot] = total
            ref = ar2.at[h, v, slot]
            steps[2, h, v] = [copies.start(ref, ref, place.device(axis, d)) for d in (1, 3, 2)]

    def sum3(h):
        for v in range(2):
            arrived(steps[2, h, v])
            total = (ar2[h, v, 0] + ar2[h, v, 1]) + (ar2[h, v, 2] + ar2[h, v, 3])
            axis = axis_of(h, v, 2)
            slot = place.c[axis]
            ar3[h, v, core, slot] = total
            ref = ar3.at[h, v, core, slot]
            steps[3, h, v] = [
                copies.start(ref, ref, place.device(axis, d, f))
                for d in (0, 1, 3, 2) for f in (False, True) if d or f
            ]

    def weigh(h):
        for v in range(2):
            arrived(steps[3, h, v])
        scale = None
        for t in range(4):
            k, lanes = t // 2, slice((t % 2) * LN, (t % 2 + 1) * LN)
            tile = jnp.concatenate(
                [
                    (ar3[h, v, k, 0, :, lanes] + ar3[h, v, k, 1, :, lanes])
                    + (ar3[h, v, k, 2, :, lanes] + ar3[h, v, k, 3, :, lanes])
                    for v in range(2)
                ],
                axis=0,
            )
            if scale is None:
                norm_sq = tile[:, MG : MG + 1]
                cells = jnp.float32(2 * 128 * BLK * BV)
                scale = jnp.sqrt(cells) * lax.rsqrt(norm_sq + 1e-06)
            tile = tile * scale
            corr[h * SH : (h + 1) * SH, t * LN : (t + 1) * LN] = tile[0:SH]
            corr[S + h * SH : S + (h + 1) * SH, t * LN : (t + 1) * LN] = tile[8 : 8 + SH]
            weights = tile / eig[0:1, t * LN : (t + 1) * LN]
            for k in range(4):
                wt[h, 4 * t + k] = spread_lanes(jnp.where(group32 == k, weights, 0.0)).astype(BF16)

    def mix(h):
        low8 = low_lanes((8, LN))
        zero = jnp.zeros((RR, LN), BF16)

        def eight(g, carry):
            strips = []
            for a in range(8):
                group = pos[g * 8 + a] & (GROUPS - 1)
                strip = jnp.where(group32 == a % 4, wt[h, group], zero)
                pair = [strip, zero] if a < 4 else [zero, strip]
                strips.append(jnp.concatenate(pair, axis=1))
            left = jnp.concatenate(strips, axis=0)
            right = modes[pl.ds(pl.multiple_of(g * 8 * MP, 8 * MP), 8 * MP), :]
            out = jnp.dot(left, right, preferred_element_type=F32)
            for a in range(8):
                real, imag = out[a * RR : a * RR + 8], out[a * RR + 8 : a * RR + 16]
                turned = pltpu.roll(imag, NB, 1)
                at = pl.ds(pl.multiple_of((g * 8 + a) * 8, 8), 8)
                tall[at, :] = real + jnp.where(low8, -turned, turned)
            return carry

        lax.fori_loop(0, RECS // 8, eight, 0, unroll=4)
        for s in range(SH):
            both[h, 0:RECS, s * LN : (s + 1) * LN] = tall[pl.ds(s, RECS, stride=8), :].astype(BF16)
        exchange["g", h] = copies.start(both.at[h, 0:RECS], both.at[h, RECS : 2 * RECS], sib)

    def partial(q, c3):
        h, p = q // 3, q % 3
        at = pl.ds(pl.multiple_of(c3 * PLANE, PLANE), PLANE)
        return jnp.dot(
            pick_t[p, at, :], both[h, :, p * PW : (p + 1) * PW], preferred_element_type=F32
        )

    far, near, lines, owns = {}, {}, {}, {}

    def rs1(q):
        a3 = order(q)[2]
        half = PLANE // 2
        far_out[q] = partial(q, place.at(a3, 2)).astype(BF16)
        far[q] = [
            copies.start(far_out.at[q, 0:half, :], far_in.at[q, 0], place.device(a3, 1)),
            copies.start(far_out.at[q, half:PLANE, :], far_in.at[q, 1], place.device(a3, 3)),
        ]

    def rs2(q):
        a3 = order(q)[2]
        half = PLANE // 2
        near[q] = []
        for k, d in enumerate((1, 3)):
            total = partial(q, place.at(a3, d))
            far[q][k].wait_recv()
            more = far_in[q, k].astype(F32)
            halves = [total[0:half], total[half:PLANE]]
            halves[k] = halves[k] + more
            near_out[q, k, 0:half, :] = halves[0].astype(BF16)
            near_out[q, k, half:PLANE, :] = halves[1].astype(BF16)
            near[q].append(copies.start(near_out.at[q, k], near_in.at[q, k], place.device(a3, d)))

    def rs_own(q):
        x[q] = partial(q, place.c[order(q)[2]])

    def line_at(axis, d, size):
        return pl.ds(pl.multiple_of(place.at(axis, d) * size, size), size)

    def rs3(q):
        a2 = order(q)[1]
        arrived(near[q])
        x[q] = x[q] + near_in[q, 0].astype(F32) + near_in[q, 1].astype(F32)
        lines[q] = []
        for k, d in enumerate((1, 3, 2)):
            line_out[q, k] = x[q, line_at(a2, d, LINE), :].astype(BF16)
            lines[q].append(copies.start(line_out.at[q, k], line_in.at[q, k], place.device(a2, d)))

    def rs4(q):
        a1, a2, _ = order(q)
        total = x[q, line_at(a2, 0, LINE), :]
        for k in range(3):
            lines[q][k].wait_recv()
            total = total + line_in[q, k].astype(F32)
        x[q, 0:LINE, :] = total
        owns[q] = []
        for k, d in enumerate((1, 3, 2)):
            own_out[q, k] = x[q, line_at(a1, d, BLK), :].astype(BF16)
            owns[q].append(copies.start(own_out.at[q, k], own_in.at[q, k], place.device(a1, d)))

    def rs5(q):
        total = x[q, line_at(order(q)[0], 0, BLK), :]
        for k in range(3):
            owns[q][k].wait_recv()
            total = total + own_in[q, k].astype(F32)
        for k in range(2):
            gs[pl.ds(q * 2 + k, BLK, stride=16), :] = total[:, k * LN : (k + 1) * LN]

    h0, h1 = (0, 1, 2), (3, 4, 5)
    for q in h0 + h1:
        ag1(q)
    idsb[0] = jnp.zeros((8, RECS), I32)
    idsb[0, 0:1, :] = owner_in[...]
    idsb[0, 1:2, :] = pos_in[...]
    id_copy = copies.start(idsb.at[0], idsb.at[1], sib)
    load_coeffs.wait()
    make_modes()
    make_tables()
    for hq in (h0, h1):
        for q in hq:
            ag2(q)
        for q in hq:
            ag3(q, 0)
    id_copy.wait_recv()
    make_keys()
    make_picks()
    for hq in (h0, h1):
        for d in (3, 1, 2):
            for q in hq:
                ag3(q, d)
    make_picks_t()
    for hq in (h0, h1):
        for d in (0, 3, 1, 2):
            for q in hq:
                ag_forward(q, d)
    gather(0)
    project(0)
    sum1(0)
    gather(1)
    project(1)
    sum2(0)
    sum1(1)
    sum3(0)
    sum2(1)
    weigh(0)
    mix(0)
    sum3(1)
    exchange["g", 0].wait_recv()
    for q in h0:
        rs1(q)
    weigh(1)
    mix(1)
    for q in h0:
        rs2(q)
    exchange["g", 1].wait_recv()
    for q in h1:
        rs1(q)
    for q in h0:
        rs_own(q)
    for q in h0:
        rs3(q)
    for q in h1:
        rs2(q)
    for q in h1:
        rs_own(q)
    for q in h0:
        rs4(q)
    for q in h1:
        rs3(q)
    for r in range(GROUPS):
        corr_out[:, r * MG : (r + 1) * MG] = corr[:, r * MP : r * MP + MG]
    for q in h0:
        rs5(q)
    for q in h1:
        rs4(q)
    for q in h1:
        rs5(q)

    def out_copy(b):
        return pltpu.make_async_copy(gout.at[b], guesses.at[b], osem.at[b])

    def guess(b, carry):
        g = gs[pl.ds(pl.multiple_of(b * 16, 16), S), :]
        comb[0:S, :] = jnp.where(low12, g, -g)
        comb[S : 2 * S, :] = pltpu.roll(g, NB, 1)
        gout[b] = jnp.dot(comb[...].astype(BF16), bbuf[b], preferred_element_type=F32).astype(BF16)
        out_copy(b).start()
        return carry

    lax.fori_loop(0, BLK, guess, 0)
    for b in range(BLK):
        out_copy(b).wait()
    copies.finish()


def shards(basis, sources, old_coeffs, eigenvalues, dest_owner, new_pos):
    hbm = pl.BlockSpec(memory_space=pl.ANY)
    vmem = pl.BlockSpec(memory_space=pltpu.VMEM)
    smem = pl.BlockSpec(memory_space=pltpu.SMEM)
    half_lanes = GROUPS * MP // 2
    guesses, correlations = pl.pallas_call(
        kernel,
        out_shape=(
            jax.ShapeDtypeStruct((BLK, 2 * S, BV), BF16),
            jax.ShapeDtypeStruct((2 * S, MODES), F32),
        ),
        in_specs=[hbm, hbm, hbm, vmem, vmem, smem, vmem],
        out_specs=(hbm, vmem),
        scratch_shapes=[
            pltpu.VMEM((BLK, LN, BV), BF16),
            pltpu.VMEM((BLK, 2 * S, BV), BF16),
            pltpu.VMEM((4 * S, 2 * LN), F32),
            pltpu.VMEM((BLK * 16, LN), F32),
            pltpu.VMEM((2 * S, LN), F32),
            pltpu.VMEM((PARTS, SAME, PW), BF16),
            pltpu.VMEM((2, 8, RECS), I32),
            pltpu.VMEM((RECS // 4, LN), F32),
            pltpu.VMEM((8, GROUPS * MP), F32),
            pltpu.VMEM((RECS // 4 * RR, LN), F32),
            pltpu.VMEM((RECS, MG * LN), BF16),
            pltpu.VMEM((LN, RECS), F32),
            pltpu.VMEM((RECS, LN), F32),
            pltpu.VMEM((3, 2, RECS, SAME), BF16),
            pltpu.VMEM((3, SAME, 2 * RECS), BF16),
            pltpu.VMEM((RECS * MP, LN), F32),
            pltpu.VMEM((RECS * MP, LN), BF16),
            pltpu.VMEM((PARTS, RECS, PW), BF16),
            pltpu.VMEM((PARTS, RECS, PW), BF16),
            pltpu.VMEM((PARTS, RECS, PW), BF16),
            pltpu.VMEM((RECS * RR, LN), F32),
            pltpu.VMEM((H, RR, GROUPS * MP), F32),
            pltpu.VMEM((H, 2, 8, 8, half_lanes), F32),
            pltpu.VMEM((H, 2, 4, 8, half_lanes), F32),
            pltpu.VMEM((H, 2, 2, 4, 8, half_lanes), F32),
            pltpu.VMEM((2 * S, GROUPS * MP), F32),
            pltpu.VMEM((H, GROUPS, RR, LN), BF16),
            pltpu.VMEM((RECS * 8, LN), F32),
            pltpu.VMEM((H, 2 * RECS, HW), BF16),
            pltpu.VMEM((PARTS, PLANE, PW), BF16),
            pltpu.VMEM((PARTS, 2, PLANE // 2, PW), BF16),
            pltpu.VMEM((PARTS, 2, PLANE, PW), BF16),
            pltpu.VMEM((PARTS, 2, PLANE, PW), BF16),
            pltpu.VMEM((PARTS, PLANE, PW), F32),
            pltpu.VMEM((PARTS, 3, LINE, PW), BF16),
            pltpu.VMEM((PARTS, 3, LINE, PW), BF16),
            pltpu.VMEM((PARTS, 3, BLK, PW), BF16),
            pltpu.VMEM((PARTS, 3, BLK, PW), BF16),
            pltpu.VMEM((BLK * 16, LN), F32),
            pltpu.VMEM((2 * S, LN), F32),
            pltpu.VMEM((BLK, 2 * S, BV), BF16),
            pltpu.SemaphoreType.DMA((BLK // 2,)),
            pltpu.SemaphoreType.DMA((BLK // 2,)),
            pltpu.SemaphoreType.DMA((BLK,)),
            pltpu.SemaphoreType.DMA,
            pltpu.SemaphoreType.DMA((N_COPIES,)),
            pltpu.SemaphoreType.DMA((N_COPIES,)),
        ],
        compiler_params=pltpu.CompilerParams(
            collective_id=1, has_side_effects=True, vmem_limit_bytes=60 * MIB
        ),
    )(
        basis, sources, old_coeffs, dest_owner.reshape(1, RECS), new_pos.reshape(1, RECS),
        new_pos, eigenvalues.reshape(1, MODES),
    )
    return guesses.astype(F32), correlations.T


def solution(mesh):
    in_specs = (
        P(("gz", "ta"), None, None),
        P(("gz", "ta"), None, None),
        P(("gz", "ta"), None),
        P(),
        P(("gz", "ta")),
        P(("gz", "ta")),
    )
    out_specs = (P(("gz", "ta"), None, None), P())
    return jax.shard_map(shards, mesh=mesh, in_specs=in_specs, out_specs=out_specs, check_vma=False)
```

```python
import jax
import jax.numpy as jnp
from jax import lax
from jax.experimental import pallas as pl
from jax.experimental.pallas import tpu as pltpu
from jax.sharding import PartitionSpec as P

F32 = jnp.float32
BF16 = jnp.bfloat16
I32 = jnp.int32
MESH = pl.DeviceIdType.MESH

NB = 64
LN = 2 * NB
BV = 3072
S = 12
BLK = 16
MG = 25
MP = 32
GROUPS = 16
RECS = 256
MODES = 400
H = 2
SH = S // H
PARTS = 3 * H
PW = 2 * LN
HW = SH * LN
RR = 16
SAME = 64 * BLK
PLANE, LINE = 16 * BLK, 4 * BLK
MIB = 1 << 20
N_COPIES = 1 + PARTS * 22 + PARTS + H * (14 + 6 + 14) + H + PARTS * 18


class Place:
    def __init__(self):
        gz = lax.axis_index("gz")
        ta = lax.axis_index("ta")
        self.core = lax.rem(gz, 2)
        self.c = (ta // 4, gz // 2, lax.rem(ta, 4))
        self.known = {}

    def at(self, axis, d):
        if (axis, d) not in self.known:
            self.known[axis, d] = lax.rem(self.c[axis] + d, 4) if d else self.c[axis]
        return self.known[axis, d]

    def device(self, axis, d, flip=False):
        if (axis, d, flip) not in self.known:
            x, y, z = (self.at(a, d) if a == axis else self.c[a] for a in range(3))
            core = 1 - self.core if flip else self.core
            self.known[axis, d, flip] = (y * 2 + core, x * 4 + z)
        return self.known[axis, d, flip]


def order(q):
    return (q % 3, (q + 1) % 3, (q + 2) % 3)


class Copies:
    def __init__(self, send, recv):
        self.send, self.recv, self.all, self.settled = send, recv, [], 0

    def start(self, src, dst, device):
        n = len(self.all)
        copy = pltpu.make_async_remote_copy(
            src_ref=src,
            dst_ref=dst,
            send_sem=self.send.at[n],
            recv_sem=self.recv.at[n],
            device_id=device,
            device_id_type=MESH,
        )
        copy.start()
        self.all.append(copy)
        return copy

    def settle(self, until=None):
        until = len(self.all) if until is None else until
        for copy in self.all[self.settled : until]:
            copy.wait_send()
        self.settled = until


def arrived(copies):
    for copy in copies:
        copy.wait_recv()


def iota(shape, axis):
    return lax.broadcasted_iota(I32, shape, axis)


def low_lanes(shape):
    return iota(shape, 1) % LN < NB


def spread_lanes(x):
    x = x + pltpu.roll(x, 2 * MP, 1)
    return x + pltpu.roll(x, MP, 1)


def kernel(
    basis, sources, coeffs_in, owner_in, pos_in, pos, eig_in,
    g_out, corr_out, bbuf,
    sbuf, prod, stage, sq, table, idsb, lane_group, eig, terms, coeffs, kbig, kcol, pick, pick_t, wide, modes,
    mine, theirs, got, xs, pay, ar1, ar2, ar3, corr, wt, tall, both,
    far_out, far_in, near_sum, near_out, near_in, x, line_out, line_in, own_out, own_in, gs,
    bsem, ssem, csem, send, recv,
):
    place = Place()
    core = place.core
    sib = place.device(0, 0, True)
    copies = Copies(send, recv)

    def pair_load(j):
        at = pl.ds(j * 2, 2)
        return (
            pltpu.make_async_copy(sources.at[at], sbuf.at[at], ssem.at[j]),
            pltpu.make_async_copy(basis.at[at], bbuf.at[at], bsem.at[j]),
        )

    for j in range(3):
        for copy in pair_load(j):
            copy.start()
    load_coeffs = pltpu.make_async_copy(coeffs_in, coeffs, csem)
    load_coeffs.start()
    barrier = pltpu.get_barrier_semaphore()
    friends = [sib] + [place.device(a, d, f) for a in range(3) for d in (1, 2, 3) for f in (False, True)]
    for friend in friends:
        pl.semaphore_signal(barrier, inc=1, device_id=friend, device_id_type=MESH)

    low12 = low_lanes((S, LN))

    def block_pair(j, total):
        for copy in pair_load(j):
            copy.wait()

        @pl.when(j + 3 < BLK // 2)
        def _():
            for copy in pair_load(j + 3):
                copy.start()

        at = pl.ds(j * 2, 2)
        field = sbuf[at].reshape(4 * S, BV)
        vectors = bbuf[at].reshape(2 * LN, BV)
        prod[...] = lax.dot_general(
            field, vectors, (((1,), (1,)), ((), ())), preferred_element_type=F32
        )
        for k in range(2):
            lanes = slice(k * LN, (k + 1) * LN)
            a = prod[2 * S * k : 2 * S * k + S, lanes]
            b = pltpu.roll(prod[2 * S * k + S : 2 * S * k + 2 * S, lanes], NB, 1)
            stage[pl.ds(pl.multiple_of((j * 2 + k) * 16, 16), S), :] = b + jnp.where(low12, a, -a)
        wide_field = field.astype(F32)
        wide_field = wide_field * wide_field
        for t in range(BV // LN):
            total = total + wide_field[:, t * LN : (t + 1) * LN]
        return total

    total = lax.fori_loop(0, BLK // 2, block_pair, jnp.zeros((4 * S, LN), F32))
    sq[...] = jnp.broadcast_to(
        jnp.sum(total[0 : 2 * S] + total[2 * S : 4 * S], axis=1, keepdims=True), (2 * S, LN)
    )
    pl.semaphore_wait(barrier, len(friends))

    def row(c3, c2, c1=0):
        return pl.multiple_of(((c3 * 4 + c2) * 4 + c1) * BLK, BLK)

    def rows(q, start, size):
        return table.at[q, pl.ds(start, size), :]

    first, second, third, last = {}, {}, {}, {}

    def to_axis(q, axis, start, size, ds):
        ref = rows(q, start, size)
        return [copies.start(ref, ref, place.device(axis, d)) for d in ds]

    def ag1(q):
        a1, a2, a3 = order(q)
        here = row(place.c[a3], place.c[a2], place.c[a1])
        s = q * 2
        own = [stage[pl.ds(s + k, BLK, stride=16), :] for k in range(2)]
        table[q, pl.ds(here, BLK), :] = jnp.concatenate(own, axis=1).astype(BF16)
        first[q] = to_axis(q, a1, here, BLK, (1, 3, 2))

    def ag2(q):
        _, a2, a3 = order(q)
        arrived(first[q])
        second[q] = to_axis(q, a2, row(place.c[a3], place.c[a2]), LINE, (1, 3, 2))

    def ag3(q, d):
        _, a2, a3 = order(q)
        if d:
            second[q][{3: 0, 1: 1, 2: 2}[d]].wait_recv()
        third[q, d] = to_axis(q, a3, row(place.c[a3], place.at(a2, d)), LINE, (1, 3))

    def ag_forward(q, d):
        _, a2, a3 = order(q)
        arrived(third[q, d])
        c2 = place.at(a2, d)
        half = LINE // 2
        a = rows(q, row(place.at(a3, 3), c2), half)
        b = rows(q, pl.multiple_of(row(place.at(a3, 1), c2) + half, BLK), half)
        last[q, d] = [
            copies.start(a, a, place.device(a3, 1)),
            copies.start(b, b, place.device(a3, 3)),
        ]

    def make_keys():
        kbig[...] = jnp.zeros_like(kbig)
        for who in range(2):
            owner, at = idsb[who, 0:1, :], idsb[who, 1:2, :]
            c = ((owner >> 2) & 3, owner >> 5, owner & 3)
            same = ((owner >> 4) & 1) == core
            for p in range(3):
                a1, a2, a3 = order(p)
                key = ((c[a3] * 4 + c[a2]) * 4 + c[a1]) * BLK + (at >> 4)
                key = jnp.where(same, key, -1)
                kbig[who * 3 + p : who * 3 + p + 1, :] = key.astype(F32)
        kcol[...] = kbig[...].T

    def make_picks():
        wide_ids = iota((RECS, SAME), 1).astype(F32)
        for who in range(2):
            for p in range(3):
                k = who * 3 + p
                pick[p, (1 - who) * RECS : (2 - who) * RECS, :] = jnp.where(kcol[:, k : k + 1] == wide_ids, 1.0, 0.0).astype(BF16)

    def make_picks_t():
        tall_ids = iota((SAME, RECS), 0).astype(F32)
        for who in range(2):
            for p in range(3):
                k = who * 3 + p
                pick_t[p, :, who * RECS : (who + 1) * RECS] = jnp.where(
                    kbig[k : k + 1, :] == tall_ids, 1.0, 0.0
                ).astype(BF16)

    def make_modes():
        for m in range(MG):
            wide[pl.ds(m, RECS, stride=MP), :] = coeffs[:, m * LN : (m + 1) * LN].astype(F32)
        for m in range(MG, MP):
            wide[pl.ds(m, RECS, stride=MP), :] = jnp.zeros((RECS, LN), F32)
        modes[...] = wide[...].astype(BF16)

    def make_tables():
        i = iota((RECS // 4, RECS), 1)
        group = jnp.where(i // 4 == iota((RECS // 4, RECS), 0), pos_in[...] & (GROUPS - 1), 0)
        lanes = iota((RECS, LN), 0) % 4 == iota((RECS, LN), 1) // MP
        lane_group[...] = jnp.dot(
            group.astype(F32).astype(BF16),
            jnp.where(lanes, 1.0, 0.0).astype(BF16),
            preferred_element_type=F32,
        )
        wide_eig = jnp.concatenate([eig_in[...], jnp.ones((1, GROUPS * MP - MODES), F32)], axis=1)
        lane = iota((1, GROUPS * MP), 1)
        padded = jnp.full((1, GROUPS * MP), jnp.inf, F32)
        for r in range(GROUPS):
            moved = pltpu.roll(wide_eig, r * (MP - MG), 1) if r else wide_eig
            padded = jnp.where((lane // MP == r) & (lane % MP < MG), moved, padded)
        eig[...] = jnp.broadcast_to(padded, eig.shape)

    exchange = {}

    def gather(h):
        for p in range(3):
            q = h * 3 + p
            for d in range(4):
                arrived(last[q, d])
            found = jnp.dot(pick[p], table[q], preferred_element_type=F32)
            theirs[q] = found[0:RECS].astype(BF16)
            exchange[q] = copies.start(theirs.at[q], got.at[q], sib)
            mine[q] = found[RECS : 2 * RECS].astype(BF16)

    low_rec = low_lanes((RECS, LN))
    group32 = iota((RR, LN), 1) // MP

    def project_start(h):
        for s in (6, 7, 14, 15):
            xs[pl.ds(s, RECS, stride=RR), :] = jnp.zeros((RECS, LN), F32)
        for p in range(3):
            q = h * 3 + p
            exchange[q].wait_recv()
            both_cores = mine[q].astype(F32) + got[q].astype(F32)
            for k in range(2):
                real = both_cores[:, k * LN : (k + 1) * LN]
                turned = pltpu.roll(real, NB, 1)
                xs[pl.ds(2 * p + k, RECS, stride=RR), :] = real
                xs[pl.ds(8 + 2 * p + k, RECS, stride=RR), :] = jnp.where(low_rec, turned, -turned)

    def project(h):
        def eight(g, carry):
            left = xs[pl.ds(pl.multiple_of(g * 8 * RR, 8 * RR), 8 * RR), :].astype(BF16)
            right = modes[pl.ds(pl.multiple_of(g * 8 * MP, 8 * MP), 8 * MP), :]
            out = lax.dot_general(left, right, (((1,), (1,)), ((), ())), preferred_element_type=F32)
            for t in range(2):
                lanes = slice(t * LN, (t + 1) * LN)
                term = out[4 * t * RR : (4 * t + 1) * RR, lanes]
                for k in range(1, 4):
                    a = 4 * t + k
                    term = jnp.where(group32 == k, out[a * RR : (a + 1) * RR, lanes], term)
                terms[pl.ds(pl.multiple_of((g * 2 + t) * RR, RR), RR), :] = term
            return carry

        lax.fori_loop(0, RECS // 8, eight, 0, unroll=8)

        def four(g, acc):
            term = terms[pl.ds(pl.multiple_of(g * RR, RR), RR), :]
            whose = lane_group[pl.ds(g, 1), :]
            return tuple(acc[r] + jnp.where(whose == float(r), term, 0.0) for r in range(GROUPS))

        acc = lax.fori_loop(0, RECS // 4, four, (jnp.zeros((RR, LN), F32),) * GROUPS, unroll=4)
        for t in range(4):
            tile = spread_lanes(acc[4 * t])
            for k in range(1, 4):
                tile = jnp.where(group32 == k, spread_lanes(acc[4 * t + k]), tile)
            pay[h, :, t * LN : (t + 1) * LN] = tile
        norm = sq[h * SH : (h + 1) * SH, :] + sq[S + h * SH : S + (h + 1) * SH, :]
        lane = iota((SH, LN), 1)
        for base in (0, 8):
            old = pay[h, base : base + SH, 0:LN]
            pay[h, base : base + SH, 0:LN] = jnp.where(lane == MG, norm, old)

    steps = {}
    half_lanes = GROUPS * MP // 2

    def axis_of(h, v, step):
        return (v + h + step) % 3

    def sum1(h):
        for v in range(2):
            axis = axis_of(h, v, 0)
            slot = place.c[axis] * 2 + core
            piece = slice(8 * v, 8 * v + 8)
            ours = pl.ds(pl.multiple_of(core * half_lanes, half_lanes), half_lanes)
            other = pl.ds(pl.multiple_of((1 - core) * half_lanes, half_lanes), half_lanes)
            ar1[h, v, slot] = pay[h, piece, ours]
            dst = ar1.at[h, v, slot]
            steps[1, h, v] = [
                copies.start(pay.at[h, piece, other if f else ours], dst, place.device(axis, d, f))
                for d in (0, 1, 3, 2) for f in (False, True) if d or f
            ]

    def sum2(h):
        for v in range(2):
            arrived(steps[1, h, v])
            total = ar1[h, v, 0]
            for k in range(1, 8):
                total = total + ar1[h, v, k]
            axis = axis_of(h, v, 1)
            slot = place.c[axis]
            ar2[h, v, slot] = total
            ref = ar2.at[h, v, slot]
            steps[2, h, v] = [copies.start(ref, ref, place.device(axis, d)) for d in (1, 3, 2)]

    def sum3(h):
        for v in range(2):
            arrived(steps[2, h, v])
            total = (ar2[h, v, 0] + ar2[h, v, 1]) + (ar2[h, v, 2] + ar2[h, v, 3])
            axis = axis_of(h, v, 2)
            slot = place.c[axis]
            ar3[h, v, core, slot] = total
            ref = ar3.at[h, v, core, slot]
            steps[3, h, v] = [
                copies.start(ref, ref, place.device(axis, d, f))
                for d in (0, 1, 3, 2) for f in (False, True) if d or f
            ]

    def weigh(h):
        for v in range(2):
            arrived(steps[3, h, v])
        scale = None
        for t in range(4):
            k, lanes = t // 2, slice((t % 2) * LN, (t % 2 + 1) * LN)
            tile = jnp.concatenate(
                [
                    (ar3[h, v, k, 0, :, lanes] + ar3[h, v, k, 1, :, lanes])
                    + (ar3[h, v, k, 2, :, lanes] + ar3[h, v, k, 3, :, lanes])
                    for v in range(2)
                ],
                axis=0,
            )
            if scale is None:
                norm_sq = tile[:, MG : MG + 1]
                cells = jnp.float32(2 * 128 * BLK * BV)
                scale = jnp.sqrt(cells) * lax.rsqrt(norm_sq + 1e-06)
            tile = tile * scale
            corr[h * SH : (h + 1) * SH, t * LN : (t + 1) * LN] = tile[0:SH]
            corr[S + h * SH : S + (h + 1) * SH, t * LN : (t + 1) * LN] = tile[8 : 8 + SH]
            weights = tile / eig[0:1, t * LN : (t + 1) * LN]
            for k in range(4):
                wt[h, 4 * t + k] = spread_lanes(jnp.where(group32 == k, weights, 0.0)).astype(BF16)

    def mix(h):
        low8 = low_lanes((8, LN))
        zero = jnp.zeros((RR, LN), BF16)

        def eight(g, carry):
            strips = []
            for a in range(8):
                group = pos[g * 8 + a] & (GROUPS - 1)
                strip = jnp.where(group32 == a % 4, wt[h, group], zero)
                pair = [strip, zero] if a < 4 else [zero, strip]
                strips.append(jnp.concatenate(pair, axis=1))
            left = jnp.concatenate(strips, axis=0)
            right = modes[pl.ds(pl.multiple_of(g * 8 * MP, 8 * MP), 8 * MP), :]
            out = jnp.dot(left, right, preferred_element_type=F32)
            for a in range(8):
                real, imag = out[a * RR : a * RR + 8], out[a * RR + 8 : a * RR + 16]
                turned = pltpu.roll(imag, NB, 1)
                at = pl.ds(pl.multiple_of((g * 8 + a) * 8, 8), 8)
                tall[at, :] = real + jnp.where(low8, -turned, turned)
            return carry

        lax.fori_loop(0, RECS // 8, eight, 0, unroll=8)
        for s in range(SH):
            both[h, 0:RECS, s * LN : (s + 1) * LN] = tall[pl.ds(s, RECS, stride=8), :].astype(BF16)
        exchange["g", h] = copies.start(both.at[h, 0:RECS], both.at[h, RECS : 2 * RECS], sib)

    def partial(q, c3):
        h, p = q // 3, q % 3
        at = pl.ds(pl.multiple_of(c3 * PLANE, PLANE), PLANE)
        return jnp.dot(
            pick_t[p, at, :], both[h, :, p * PW : (p + 1) * PW], preferred_element_type=F32
        )

    far, near, lines, owns = {}, {}, {}, {}

    by_side = ((2, 1), (3, 0))

    def line_at(axis, d, size):
        return pl.ds(pl.multiple_of(place.at(axis, d) * size, size), size)

    def rs1(q):
        _, a2, a3 = order(q)
        far_out[q] = partial(q, place.at(a3, 2)).astype(BF16)
        for k, d in enumerate((1, 3)):
            for j, n in enumerate(by_side[k]):
                far[q, k, j] = copies.start(
                    far_out.at[q, line_at(a2, n, LINE), :], far_in.at[q, k, j], place.device(a3, d)
                )

    def send_near(q, k, n):
        _, a2, a3 = order(q)
        near[q, k, n] = copies.start(
            near_out.at[q, k, line_at(a2, n, LINE), :],
            near_in.at[q, k, n],
            place.device(a3, (1, 3)[k]),
        )

    def rs_near(q):
        _, a2, a3 = order(q)
        for k, d in enumerate((1, 3)):
            near_sum[q, k] = partial(q, place.at(a3, d))
            for n in by_side[1 - k]:
                at = line_at(a2, n, LINE)
                near_out[q, k, at, :] = near_sum[q, k, at, :].astype(BF16)
                send_near(q, k, n)

    def rs2(q):
        a2 = order(q)[1]
        for k in range(2):
            for j, n in enumerate(by_side[k]):
                far[q, k, j].wait_recv()
                at = line_at(a2, n, LINE)
                total = near_sum[q, k, at, :] + far_in[q, k, j].astype(F32)
                near_out[q, k, at, :] = total.astype(BF16)
                send_near(q, k, n)

    def rs_own(q):
        x[q] = partial(q, place.c[order(q)[2]])

    def whole_line(q, n):
        total = x[q, line_at(order(q)[1], n, LINE), :]
        for k in range(2):
            near[q, k, n].wait_recv()
            total = total + near_in[q, k, n].astype(F32)
        return total

    def rs3(q):
        a2 = order(q)[1]
        for n in (2, 1, 3):
            line_out[q, n - 1] = whole_line(q, n).astype(BF16)
            lines[q, n] = copies.start(
                line_out.at[q, n - 1], line_in.at[q, n - 1], place.device(a2, n)
            )

    def rs4(q):
        a1 = order(q)[0]
        total = whole_line(q, 0)
        for n in (1, 3, 2):
            lines[q, n].wait_recv()
            total = total + line_in[q, n - 1].astype(F32)
        x[q, 0:LINE, :] = total
        owns[q] = []
        for k, d in enumerate((1, 3, 2)):
            own_out[q, k] = x[q, line_at(a1, d, BLK), :].astype(BF16)
            owns[q].append(copies.start(own_out.at[q, k], own_in.at[q, k], place.device(a1, d)))

    def rs5(q):
        total = x[q, line_at(order(q)[0], 0, BLK), :]
        for k in range(3):
            owns[q][k].wait_recv()
            total = total + own_in[q, k].astype(F32)
        for k in range(2):
            gs[pl.ds(q * 2 + k, BLK, stride=16), :] = total[:, k * LN : (k + 1) * LN]

    h0, h1 = (0, 1, 2), (3, 4, 5)
    for q in h0 + h1:
        ag1(q)
    idsb[0] = jnp.zeros((8, RECS), I32)
    idsb[0, 0:1, :] = owner_in[...]
    idsb[0, 1:2, :] = pos_in[...]
    id_copy = copies.start(idsb.at[0], idsb.at[1], sib)
    load_coeffs.wait()
    make_modes()
    make_tables()
    for hq in (h0, h1):
        for q in hq:
            ag2(q)
        for q in hq:
            ag3(q, 0)
    id_copy.wait_recv()
    make_keys()
    make_picks()
    for hq in (h0, h1):
        for d in (3, 1, 2):
            for q in hq:
                ag3(q, d)
    make_picks_t()
    for d in (0, 3, 1, 2):
        for q in h0:
            ag_forward(q, d)
    for q in h1:
        ag_forward(q, 0)
    gather(0)
    for d in (3, 1):
        for q in h1:
            ag_forward(q, d)
    project_start(0)
    for q in h1:
        ag_forward(q, 2)
    project(0)
    sum1(0)
    gather(1)
    project_start(1)
    project(1)
    sum1(1)
    sum2(0)
    sum3(0)
    sum2(1)
    sum3(1)
    weigh(0)
    mix(0)
    exchange["g", 0].wait_recv()
    for q in h0:
        rs1(q)
    for q in h0:
        rs_near(q)
    for q in h0:
        rs_own(q)
    weigh(1)
    mix(1)
    for q in h0:
        rs2(q)
    exchange["g", 1].wait_recv()
    for q in h1:
        rs1(q)
    for q in h1:
        rs_near(q)
    for q in h1:
        rs_own(q)
    far_sent = len(copies.all)
    for q in h1:
        rs2(q)
    copies.settle(far_sent)
    for q in h0:
        rs3(q)
    for r in range(GROUPS):
        corr_out[:, r * MG : (r + 1) * MG] = corr[:, r * MP : r * MP + MG]
    for q in h1:
        rs3(q)
    for q in h0:
        rs4(q)
    copies.settle()
    for q in h1:
        rs4(q)
    for q in h0 + h1:
        rs5(q)
    g_out[...] = gs[...]
    copies.settle()


def guess_kernel(g_in, corr_in, bbuf, guesses, corr_out, comb, gout, osem):
    corr_out[...] = corr_in[...]
    low12 = low_lanes((S, LN))

    def out_copy(j):
        at = pl.ds(j * 2, 2)
        return pltpu.make_async_copy(gout.at[at], guesses.at[at], osem.at[j])

    def guess(j, carry):
        for k in range(2):
            g = g_in[pl.ds(pl.multiple_of((j * 2 + k) * 16, 16), S), :]
            lanes = slice(k * LN, (k + 1) * LN)
            comb[2 * S * k : 2 * S * k + S, lanes] = jnp.where(low12, g, -g)
            comb[2 * S * k + S : 2 * S * (k + 1), lanes] = pltpu.roll(g, NB, 1)
        vectors = bbuf[pl.ds(j * 2, 2)].reshape(2 * LN, BV)
        out = jnp.dot(comb[...].astype(BF16), vectors, preferred_element_type=F32)
        gout[j * 2] = out[0 : 2 * S]
        gout[j * 2 + 1] = out[2 * S : 4 * S]
        out_copy(j).start()
        return carry

    comb[...] = jnp.zeros_like(comb)
    lax.fori_loop(0, BLK // 2, guess, 0, unroll=2)
    for j in range(BLK // 2):
        out_copy(j).wait()


def shards(basis, sources, old_coeffs, eigenvalues, dest_owner, new_pos):
    hbm = pl.BlockSpec(memory_space=pl.ANY)
    vmem = pl.BlockSpec(memory_space=pltpu.VMEM)
    smem = pl.BlockSpec(memory_space=pltpu.SMEM)
    half_lanes = GROUPS * MP // 2
    g, corr, vectors = pl.pallas_call(
        kernel,
        out_shape=(
            pltpu.VMEM((BLK * 16, LN), F32),
            pltpu.VMEM((2 * S, MODES), F32),
            pltpu.VMEM((BLK, LN, BV), BF16),
        ),
        in_specs=[hbm, hbm, hbm, vmem, vmem, smem, vmem],
        out_specs=(vmem, vmem, vmem),
        scratch_shapes=[
            pltpu.VMEM((BLK, 2 * S, BV), BF16),
            pltpu.VMEM((4 * S, 2 * LN), F32),
            pltpu.VMEM((BLK * 16, LN), F32),
            pltpu.VMEM((2 * S, LN), F32),
            pltpu.VMEM((PARTS, SAME, PW), BF16),
            pltpu.VMEM((2, 8, RECS), I32),
            pltpu.VMEM((RECS // 4, LN), F32),
            pltpu.VMEM((8, GROUPS * MP), F32),
            pltpu.VMEM((RECS // 4 * RR, LN), F32),
            pltpu.VMEM((RECS, MG * LN), BF16),
            pltpu.VMEM((LN, RECS), F32),
            pltpu.VMEM((RECS, LN), F32),
            pltpu.VMEM((3, 2 * RECS, SAME), BF16),
            pltpu.VMEM((3, SAME, 2 * RECS), BF16),
            pltpu.VMEM((RECS * MP, LN), F32),
            pltpu.VMEM((RECS * MP, LN), BF16),
            pltpu.VMEM((PARTS, RECS, PW), BF16),
            pltpu.VMEM((PARTS, RECS, PW), BF16),
            pltpu.VMEM((PARTS, RECS, PW), BF16),
            pltpu.VMEM((RECS * RR, LN), F32),
            pltpu.VMEM((H, RR, GROUPS * MP), F32),
            pltpu.VMEM((H, 2, 8, 8, half_lanes), F32),
            pltpu.VMEM((H, 2, 4, 8, half_lanes), F32),
            pltpu.VMEM((H, 2, 2, 4, 8, half_lanes), F32),
            pltpu.VMEM((2 * S, GROUPS * MP), F32),
            pltpu.VMEM((H, GROUPS, RR, LN), BF16),
            pltpu.VMEM((RECS * 8, LN), F32),
            pltpu.VMEM((H, 2 * RECS, HW), BF16),
            pltpu.VMEM((PARTS, PLANE, PW), BF16),
            pltpu.VMEM((PARTS, 2, 2, LINE, PW), BF16),
            pltpu.VMEM((PARTS, 2, PLANE, PW), F32),
            pltpu.VMEM((PARTS, 2, PLANE, PW), BF16),
            pltpu.VMEM((PARTS, 2, 4, LINE, PW), BF16),
            pltpu.VMEM((PARTS, PLANE, PW), F32),
            pltpu.VMEM((PARTS, 3, LINE, PW), BF16),
            pltpu.VMEM((PARTS, 3, LINE, PW), BF16),
            pltpu.VMEM((PARTS, 3, BLK, PW), BF16),
            pltpu.VMEM((PARTS, 3, BLK, PW), BF16),
            pltpu.VMEM((BLK * 16, LN), F32),
            pltpu.SemaphoreType.DMA((BLK // 2,)),
            pltpu.SemaphoreType.DMA((BLK // 2,)),
            pltpu.SemaphoreType.DMA,
            pltpu.SemaphoreType.DMA((N_COPIES,)),
            pltpu.SemaphoreType.DMA((N_COPIES,)),
        ],
        compiler_params=pltpu.CompilerParams(
            collective_id=1, has_side_effects=True, vmem_limit_bytes=46 * MIB
        ),
    )(
        basis, sources, old_coeffs, dest_owner.reshape(1, RECS), new_pos.reshape(1, RECS),
        new_pos, eigenvalues.reshape(1, MODES),
    )
    guesses, correlations = pl.pallas_call(
        guess_kernel,
        out_shape=(
            jax.ShapeDtypeStruct((BLK, 2 * S, BV), F32),
            jax.ShapeDtypeStruct((2 * S, MODES), F32),
        ),
        in_specs=[vmem, vmem, vmem],
        out_specs=(hbm, vmem),
        scratch_shapes=[
            pltpu.VMEM((4 * S, 2 * LN), F32),
            pltpu.VMEM((BLK, 2 * S, BV), F32),
            pltpu.SemaphoreType.DMA((BLK // 2,)),
        ],
        compiler_params=pltpu.CompilerParams(vmem_limit_bytes=16 * MIB),
    )(g, corr, vectors)
    return guesses, correlations.T


def solution(mesh):
    in_specs = (
        P(("gz", "ta"), None, None),
        P(("gz", "ta"), None, None),
        P(("gz", "ta"), None),
        P(),
        P(("gz", "ta")),
        P(("gz", "ta")),
    )
    out_specs = (P(("gz", "ta"), None, None), P())
    return jax.shard_map(shards, mesh=mesh, in_specs=in_specs, out_specs=out_specs, check_vma=False)
```

```python
import jax
import jax.numpy as jnp
from jax import lax
from jax.experimental import pallas as pl
from jax.experimental.pallas import tpu as pltpu
from jax.sharding import PartitionSpec as P

F32 = jnp.float32
BF16 = jnp.bfloat16
I32 = jnp.int32
MESH = pl.DeviceIdType.MESH

NB = 64
LN = 2 * NB
BV = 3072
S = 12
BLK = 16
MG = 25
MP = 32
GROUPS = 16
RECS = 256
MODES = 400
H = 2
SH = S // H
PARTS = 3 * H
PW = 2 * LN
HW = SH * LN
RR = 16
SAME = 64 * BLK
PLANE, LINE = 16 * BLK, 4 * BLK
MIB = 1 << 20
N_COPIES = 1 + PARTS * 22 + PARTS + H * (14 + 6 + 14) + 2 * H + PARTS * 18


class Place:
    def __init__(self):
        gz = lax.axis_index("gz")
        ta = lax.axis_index("ta")
        self.core = lax.rem(gz, 2)
        self.c = (ta // 4, gz // 2, lax.rem(ta, 4))
        self.known = {}

    def at(self, axis, d):
        if (axis, d) not in self.known:
            self.known[axis, d] = lax.rem(self.c[axis] + d, 4) if d else self.c[axis]
        return self.known[axis, d]

    def device(self, axis, d, flip=False):
        if (axis, d, flip) not in self.known:
            x, y, z = (self.at(a, d) if a == axis else self.c[a] for a in range(3))
            core = 1 - self.core if flip else self.core
            self.known[axis, d, flip] = (y * 2 + core, x * 4 + z)
        return self.known[axis, d, flip]


def order(q):
    return (q % 3, (q + 1) % 3, (q + 2) % 3)


class Copies:
    def __init__(self, send, recv):
        self.send, self.recv, self.all, self.settled = send, recv, [], 0

    def start(self, src, dst, device):
        n = len(self.all)
        copy = pltpu.make_async_remote_copy(
            src_ref=src,
            dst_ref=dst,
            send_sem=self.send.at[n],
            recv_sem=self.recv.at[n],
            device_id=device,
            device_id_type=MESH,
        )
        copy.start()
        self.all.append(copy)
        return copy

    def settle(self, until=None):
        until = len(self.all) if until is None else until
        for copy in self.all[self.settled : until]:
            copy.wait_send()
        self.settled = until


def arrived(copies):
    for copy in copies:
        copy.wait_recv()


def iota(shape, axis):
    return lax.broadcasted_iota(I32, shape, axis)


def low_lanes(shape):
    return iota(shape, 1) % LN < NB


def spread_lanes(x):
    x = x + pltpu.roll(x, 2 * MP, 1)
    return x + pltpu.roll(x, MP, 1)


def kernel(
    basis, sources, coeffs_in, owner_hbm, pos_hbm, pos_flat, eig_hbm,
    g_out, corr_out, bbuf,
    owner_in, pos_in, pos, eig_in, sbuf, prod, stage, sq, table, idsb, lane_group, eig, terms, coeffs, kbig, kcol, pick, pick_t, wide, modes,
    mine, theirs, got, xs, pay, ar1, ar2, ar3, corr, wt, tall, both,
    far_out, far_in, near_sum, near_out, near_in, x, line_out, line_in, own_out, own_in, gs,
    bsem, ssem, csem, isem, send, recv,
):
    place = Place()
    core = place.core
    sib = place.device(0, 0, True)
    copies = Copies(send, recv)

    def pair_load(j):
        at = pl.ds(j * 2, 2)
        return (
            pltpu.make_async_copy(sources.at[at], sbuf.at[at], ssem.at[j]),
            pltpu.make_async_copy(basis.at[at], bbuf.at[at], bsem.at[j]),
        )

    for j in range(3):
        for copy in pair_load(j):
            copy.start()
    load_coeffs = pltpu.make_async_copy(coeffs_in, coeffs, csem)
    load_coeffs.start()
    small_loads = [
        pltpu.make_async_copy(src, dst, isem.at[k])
        for k, (src, dst) in enumerate(
            ((owner_hbm, owner_in), (pos_hbm, pos_in), (pos_flat, pos), (eig_hbm, eig_in))
        )
    ]
    for copy in small_loads:
        copy.start()
    barrier = pltpu.get_barrier_semaphore()
    friends = [sib] + [place.device(a, d, f) for a in range(3) for d in (1, 2, 3) for f in (False, True)]
    for friend in friends:
        pl.semaphore_signal(barrier, inc=1, device_id=friend, device_id_type=MESH)

    low12 = low_lanes((S, LN))

    def block_pair(j, total):
        for copy in pair_load(j):
            copy.wait()

        @pl.when(j + 3 < BLK // 2)
        def _():
            for copy in pair_load(j + 3):
                copy.start()

        at = pl.ds(j * 2, 2)
        field = sbuf[at].reshape(4 * S, BV)
        vectors = bbuf[at].reshape(2 * LN, BV)
        prod[...] = lax.dot_general(
            field, vectors, (((1,), (1,)), ((), ())), preferred_element_type=F32
        )
        for k in range(2):
            lanes = slice(k * LN, (k + 1) * LN)
            a = prod[2 * S * k : 2 * S * k + S, lanes]
            b = pltpu.roll(prod[2 * S * k + S : 2 * S * k + 2 * S, lanes], NB, 1)
            stage[pl.ds(pl.multiple_of((j * 2 + k) * 16, 16), S), :] = b + jnp.where(low12, a, -a)
        wide_field = field.astype(F32)
        wide_field = wide_field * wide_field
        for t in range(BV // LN):
            total = total + wide_field[:, t * LN : (t + 1) * LN]
        return total

    total = lax.fori_loop(0, BLK // 2, block_pair, jnp.zeros((4 * S, LN), F32))
    pl.semaphore_wait(barrier, len(friends))

    def row(c3, c2, c1=0):
        return pl.multiple_of(((c3 * 4 + c2) * 4 + c1) * BLK, BLK)

    def rows(q, start, size):
        return table.at[q, pl.ds(start, size), :]

    first, second, third, last = {}, {}, {}, {}

    def to_axis(q, axis, start, size, ds):
        ref = rows(q, start, size)
        return [copies.start(ref, ref, place.device(axis, d)) for d in ds]

    def ag1(q):
        a1, a2, a3 = order(q)
        here = row(place.c[a3], place.c[a2], place.c[a1])
        s = q * 2
        own = [stage[pl.ds(s + k, BLK, stride=16), :] for k in range(2)]
        table[q, pl.ds(here, BLK), :] = jnp.concatenate(own, axis=1).astype(BF16)
        first[q] = to_axis(q, a1, here, BLK, (1, 3, 2))

    def ag2(q):
        _, a2, a3 = order(q)
        arrived(first[q])
        second[q] = to_axis(q, a2, row(place.c[a3], place.c[a2]), LINE, (1, 3, 2))

    def ag3(q, d):
        _, a2, a3 = order(q)
        if d:
            second[q][{3: 0, 1: 1, 2: 2}[d]].wait_recv()
        third[q, d] = to_axis(q, a3, row(place.c[a3], place.at(a2, d)), LINE, (1, 3))

    def ag_forward(q, d):
        _, a2, a3 = order(q)
        arrived(third[q, d])
        c2 = place.at(a2, d)
        half = LINE // 2
        a = rows(q, row(place.at(a3, 3), c2), half)
        b = rows(q, pl.multiple_of(row(place.at(a3, 1), c2) + half, BLK), half)
        last[q, d] = [
            copies.start(a, a, place.device(a3, 1)),
            copies.start(b, b, place.device(a3, 3)),
        ]

    def make_keys():
        kbig[...] = jnp.zeros_like(kbig)
        for who in range(2):
            owner, at = idsb[who, 0:1, :], idsb[who, 1:2, :]
            c = ((owner >> 2) & 3, owner >> 5, owner & 3)
            same = ((owner >> 4) & 1) == core
            for p in range(3):
                a1, a2, a3 = order(p)
                key = ((c[a3] * 4 + c[a2]) * 4 + c[a1]) * BLK + (at >> 4)
                key = jnp.where(same, key, -1)
                kbig[who * 3 + p : who * 3 + p + 1, :] = key.astype(F32)
        kcol[...] = kbig[...].T

    def make_picks():
        wide_ids = iota((RECS, SAME), 1).astype(F32)
        for who in range(2):
            for p in range(3):
                k = who * 3 + p
                pick[p, (1 - who) * RECS : (2 - who) * RECS, :] = jnp.where(kcol[:, k : k + 1] == wide_ids, 1.0, 0.0).astype(BF16)

    def make_picks_t():
        tall_ids = iota((SAME, RECS), 0).astype(F32)
        for who in range(2):
            for p in range(3):
                k = who * 3 + p
                pick_t[p, :, who * RECS : (who + 1) * RECS] = jnp.where(
                    kbig[k : k + 1, :] == tall_ids, 1.0, 0.0
                ).astype(BF16)

    def make_modes():
        for m in range(MG):
            wide[pl.ds(m, RECS, stride=MP), :] = coeffs[:, m * LN : (m + 1) * LN].astype(F32)
        for m in range(MG, MP):
            wide[pl.ds(m, RECS, stride=MP), :] = jnp.zeros((RECS, LN), F32)
        modes[...] = wide[...].astype(BF16)

    def make_tables():
        i = iota((RECS // 4, RECS), 1)
        group = jnp.where(i // 4 == iota((RECS // 4, RECS), 0), pos_in[...] & (GROUPS - 1), 0)
        lanes = iota((RECS, LN), 0) % 4 == iota((RECS, LN), 1) // MP
        lane_group[...] = jnp.dot(
            group.astype(F32).astype(BF16),
            jnp.where(lanes, 1.0, 0.0).astype(BF16),
            preferred_element_type=F32,
        )
        wide_eig = jnp.concatenate([eig_in[...], jnp.ones((1, GROUPS * MP - MODES), F32)], axis=1)
        lane = iota((1, GROUPS * MP), 1)
        padded = jnp.full((1, GROUPS * MP), jnp.inf, F32)
        for r in range(GROUPS):
            moved = pltpu.roll(wide_eig, r * (MP - MG), 1) if r else wide_eig
            padded = jnp.where((lane // MP == r) & (lane % MP < MG), moved, padded)
        eig[...] = jnp.broadcast_to(padded, eig.shape)

    exchange = {}

    def gather(h):
        for p in range(3):
            q = h * 3 + p
            for d in range(4):
                arrived(last[q, d])
            found = jnp.dot(pick[p, 0:RECS], table[q], preferred_element_type=F32)
            theirs[q] = found.astype(BF16)
            exchange[q] = copies.start(theirs.at[q], got.at[q], sib)
        for p in range(3):
            q = h * 3 + p
            found = jnp.dot(pick[p, RECS : 2 * RECS], table[q], preferred_element_type=F32)
            mine[q] = found.astype(BF16)

    low_rec = low_lanes((RECS, LN))
    group32 = iota((RR, LN), 1) // MP

    def project_start(h):
        for p in range(3):
            q = h * 3 + p
            exchange[q].wait_recv()
            both_cores = mine[q].astype(F32) + got[q].astype(F32)
            for k in range(2):
                real = both_cores[:, k * LN : (k + 1) * LN]
                turned = pltpu.roll(real, NB, 1)
                xs[pl.ds(2 * p + k, RECS, stride=RR), :] = real
                xs[pl.ds(8 + 2 * p + k, RECS, stride=RR), :] = jnp.where(low_rec, turned, -turned)

    def project(h):
        def eight(g, carry):
            left = xs[pl.ds(pl.multiple_of(g * 8 * RR, 8 * RR), 8 * RR), :].astype(BF16)
            right = modes[pl.ds(pl.multiple_of(g * 8 * MP, 8 * MP), 8 * MP), :]
            out = lax.dot_general(left, right, (((1,), (1,)), ((), ())), preferred_element_type=F32)
            for t in range(2):
                lanes = slice(t * LN, (t + 1) * LN)
                term = out[4 * t * RR : (4 * t + 1) * RR, lanes]
                for k in range(1, 4):
                    a = 4 * t + k
                    term = jnp.where(group32 == k, out[a * RR : (a + 1) * RR, lanes], term)
                terms[pl.ds(pl.multiple_of((g * 2 + t) * RR, RR), RR), :] = term
            return carry

        lax.fori_loop(0, RECS // 8, eight, 0, unroll=8)

        def four(g, acc):
            term = terms[pl.ds(pl.multiple_of(g * RR, RR), RR), :]
            whose = lane_group[pl.ds(g, 1), :]
            return tuple(acc[r] + jnp.where(whose == float(r), term, 0.0) for r in range(GROUPS))

        acc = lax.fori_loop(0, RECS // 4, four, (jnp.zeros((RR, LN), F32),) * GROUPS, unroll=4)
        for t in range(4):
            tile = spread_lanes(acc[4 * t])
            for k in range(1, 4):
                tile = jnp.where(group32 == k, spread_lanes(acc[4 * t + k]), tile)
            pay[h, :, t * LN : (t + 1) * LN] = tile
        norm = sq[h * SH : (h + 1) * SH, :] + sq[S + h * SH : S + (h + 1) * SH, :]
        lane = iota((SH, LN), 1)
        for base in (0, 8):
            old = pay[h, base : base + SH, 0:LN]
            pay[h, base : base + SH, 0:LN] = jnp.where(lane == MG, norm, old)

    steps = {}
    half_lanes = GROUPS * MP // 2

    def axis_of(h, v, step):
        return (v + h + step) % 3

    def sum1(h):
        for v in range(2):
            axis = axis_of(h, v, 0)
            slot = place.c[axis] * 2 + core
            piece = slice(8 * v, 8 * v + 8)
            ours = pl.ds(pl.multiple_of(core * half_lanes, half_lanes), half_lanes)
            other = pl.ds(pl.multiple_of((1 - core) * half_lanes, half_lanes), half_lanes)
            ar1[h, v, slot] = pay[h, piece, ours]
            dst = ar1.at[h, v, slot]
            steps[1, h, v] = [
                copies.start(pay.at[h, piece, other if f else ours], dst, place.device(axis, d, f))
                for d in (0, 1, 3, 2) for f in (False, True) if d or f
            ]

    def sum2(h):
        for v in range(2):
            arrived(steps[1, h, v])
            total = ar1[h, v, 0]
            for k in range(1, 8):
                total = total + ar1[h, v, k]
            axis = axis_of(h, v, 1)
            slot = place.c[axis]
            ar2[h, v, slot] = total
            ref = ar2.at[h, v, slot]
            steps[2, h, v] = [copies.start(ref, ref, place.device(axis, d)) for d in (1, 3, 2)]

    def sum3(h):
        for v in range(2):
            arrived(steps[2, h, v])
            total = (ar2[h, v, 0] + ar2[h, v, 1]) + (ar2[h, v, 2] + ar2[h, v, 3])
            axis = axis_of(h, v, 2)
            slot = place.c[axis]
            ar3[h, v, core, slot] = total
            ref = ar3.at[h, v, core, slot]
            steps[3, h, v] = [
                copies.start(ref, ref, place.device(axis, d, f))
                for d in (0, 1, 3, 2) for f in (False, True) if d or f
            ]

    def weigh(h):
        for v in range(2):
            arrived(steps[3, h, v])
        scale = None
        for t in range(4):
            k, lanes = t // 2, slice((t % 2) * LN, (t % 2 + 1) * LN)
            tile = jnp.concatenate(
                [
                    (ar3[h, v, k, 0, :, lanes] + ar3[h, v, k, 1, :, lanes])
                    + (ar3[h, v, k, 2, :, lanes] + ar3[h, v, k, 3, :, lanes])
                    for v in range(2)
                ],
                axis=0,
            )
            if scale is None:
                norm_sq = tile[:, MG : MG + 1]
                cells = jnp.float32(2 * 128 * BLK * BV)
                scale = jnp.sqrt(cells) * lax.rsqrt(norm_sq + 1e-06)
            tile = tile * scale
            corr[h * SH : (h + 1) * SH, t * LN : (t + 1) * LN] = tile[0:SH]
            corr[S + h * SH : S + (h + 1) * SH, t * LN : (t + 1) * LN] = tile[8 : 8 + SH]
            weights = tile / eig[0:1, t * LN : (t + 1) * LN]
            for k in range(4):
                wt[h, 4 * t + k] = spread_lanes(jnp.where(group32 == k, weights, 0.0)).astype(BF16)

    def mix(h):
        low8 = low_lanes((8, LN))
        zero = jnp.zeros((RR, LN), BF16)

        def eight(g, carry):
            strips = []
            for a in range(8):
                group = pos[g * 8 + a] & (GROUPS - 1)
                strip = jnp.where(group32 == a % 4, wt[h, group], zero)
                pair = [strip, zero] if a < 4 else [zero, strip]
                strips.append(jnp.concatenate(pair, axis=1))
            left = jnp.concatenate(strips, axis=0)
            right = modes[pl.ds(pl.multiple_of(g * 8 * MP, 8 * MP), 8 * MP), :]
            out = jnp.dot(left, right, preferred_element_type=F32)
            for a in range(8):
                real, imag = out[a * RR : a * RR + 8], out[a * RR + 8 : a * RR + 16]
                turned = pltpu.roll(imag, NB, 1)
                at = pl.ds(pl.multiple_of((g * 8 + a) * 8, 8), 8)
                tall[at, :] = real + jnp.where(low8, -turned, turned)
            return carry

        half = RECS // 2
        exchange["g", h] = []
        for k in range(2):
            lax.fori_loop(k * half // 8, (k + 1) * half // 8, eight, 0, unroll=8)
            ours = slice(k * half, (k + 1) * half)
            for s in range(SH):
                part = tall[pl.ds(k * half * 8 + s, half, stride=8), :]
                both[h, ours, s * LN : (s + 1) * LN] = part.astype(BF16)
            away = both.at[h, RECS + k * half : RECS + (k + 1) * half]
            exchange["g", h].append(copies.start(both.at[h, ours], away, sib))

    def partial(q, c3):
        h, p = q // 3, q % 3
        at = pl.ds(pl.multiple_of(c3 * PLANE, PLANE), PLANE)
        return jnp.dot(
            pick_t[p, at, :], both[h, :, p * PW : (p + 1) * PW], preferred_element_type=F32
        )

    far, near, lines, owns = {}, {}, {}, {}

    by_side = ((2, 1), (3, 0))

    def line_at(axis, d, size):
        return pl.ds(pl.multiple_of(place.at(axis, d) * size, size), size)

    def rs1(q):
        _, a2, a3 = order(q)
        far_out[q] = partial(q, place.at(a3, 2)).astype(BF16)
        for k, d in enumerate((1, 3)):
            for j, n in enumerate(by_side[k]):
                far[q, k, j] = copies.start(
                    far_out.at[q, line_at(a2, n, LINE), :], far_in.at[q, k, j], place.device(a3, d)
                )

    def send_near(q, k, n):
        _, a2, a3 = order(q)
        near[q, k, n] = copies.start(
            near_out.at[q, k, line_at(a2, n, LINE), :],
            near_in.at[q, k, n],
            place.device(a3, (1, 3)[k]),
        )

    def rs_near(q):
        _, a2, a3 = order(q)
        for k, d in enumerate((1, 3)):
            near_sum[q, k] = partial(q, place.at(a3, d))
            for n in by_side[1 - k]:
                at = line_at(a2, n, LINE)
                near_out[q, k, at, :] = near_sum[q, k, at, :].astype(BF16)
                send_near(q, k, n)

    def rs2(q):
        a2 = order(q)[1]
        for k in range(2):
            for j, n in enumerate(by_side[k]):
                far[q, k, j].wait_recv()
                at = line_at(a2, n, LINE)
                total = near_sum[q, k, at, :] + far_in[q, k, j].astype(F32)
                near_out[q, k, at, :] = total.astype(BF16)
                send_near(q, k, n)

    def rs_own(q):
        x[q] = partial(q, place.c[order(q)[2]])

    def whole_line(q, n):
        total = x[q, line_at(order(q)[1], n, LINE), :]
        for k in range(2):
            near[q, k, n].wait_recv()
            total = total + near_in[q, k, n].astype(F32)
        return total

    def rs3(q):
        a2 = order(q)[1]
        for n in (2, 1, 3):
            line_out[q, n - 1] = whole_line(q, n).astype(BF16)
            lines[q, n] = copies.start(
                line_out.at[q, n - 1], line_in.at[q, n - 1], place.device(a2, n)
            )

    def rs4(q):
        a1 = order(q)[0]
        total = whole_line(q, 0)
        for n in (1, 3, 2):
            lines[q, n].wait_recv()
            total = total + line_in[q, n - 1].astype(F32)
        x[q, 0:LINE, :] = total
        owns[q] = []
        for k, d in enumerate((1, 3, 2)):
            own_out[q, k] = x[q, line_at(a1, d, BLK), :].astype(BF16)
            owns[q].append(copies.start(own_out.at[q, k], own_in.at[q, k], place.device(a1, d)))

    def rs5(q):
        total = x[q, line_at(order(q)[0], 0, BLK), :]
        for k in range(3):
            owns[q][k].wait_recv()
            total = total + own_in[q, k].astype(F32)
        for k in range(2):
            gs[pl.ds(q * 2 + k, BLK, stride=16), :] = total[:, k * LN : (k + 1) * LN]

    h0, h1 = (0, 1, 2), (3, 4, 5)
    for q in h0 + h1:
        ag1(q)
    sq[...] = jnp.broadcast_to(
        jnp.sum(total[0 : 2 * S] + total[2 * S : 4 * S], axis=1, keepdims=True), (2 * S, LN)
    )
    for copy in small_loads:
        copy.wait()
    idsb[0] = jnp.zeros((8, RECS), I32)
    idsb[0, 0:1, :] = owner_in[...]
    idsb[0, 1:2, :] = pos_in[...]
    id_copy = copies.start(idsb.at[0], idsb.at[1], sib)
    load_coeffs.wait()
    make_modes()
    make_tables()
    for s in (6, 7, 14, 15):
        xs[pl.ds(s, RECS, stride=RR), :] = jnp.zeros((RECS, LN), F32)
    for hq in (h0, h1):
        for q in hq:
            ag2(q)
        for q in hq:
            ag3(q, 0)
    id_copy.wait_recv()
    make_keys()
    make_picks()
    for hq in (h0, h1):
        for d in (3, 1, 2):
            for q in hq:
                ag3(q, d)
    make_picks_t()
    for d in (0, 3, 1, 2):
        for q in h0:
            ag_forward(q, d)
    for q in h1:
        ag_forward(q, 0)
    gather(0)
    for d in (3, 1):
        for q in h1:
            ag_forward(q, d)
    project_start(0)
    for q in h1:
        ag_forward(q, 2)
    project(0)
    sum1(0)
    gather(1)
    project_start(1)
    sum2(0)
    project(1)
    sum1(1)
    sum3(0)
    sum2(1)
    weigh(0)
    mix(0)
    sum3(1)
    arrived(exchange["g", 0])
    for q in h0:
        rs1(q)
    for q in h0:
        rs_near(q)
    weigh(1)
    mix(1)
    for q in h0:
        rs2(q)
    arrived(exchange["g", 1])
    for q in h1:
        rs1(q)
    for q in h1:
        rs_near(q)
    for q in h0 + h1:
        rs_own(q)
    for q in h0:
        rs3(q)
    far_sent = len(copies.all)
    for q in h1:
        rs2(q)
    copies.settle(far_sent)
    for r in range(GROUPS):
        corr_out[:, r * MG : (r + 1) * MG] = corr[:, r * MP : r * MP + MG]
    for q in h1:
        rs3(q)
    for q in h0:
        rs4(q)
    copies.settle()
    for q in h1:
        rs4(q)
    for q in h0 + h1:
        rs5(q)
    g_out[...] = gs[...]
    copies.settle()


def guess_kernel(g_in, corr_in, bbuf, guesses, corr_out, comb, gout, osem):
    corr_out[...] = corr_in[...]
    low12 = low_lanes((S, LN))

    def out_copy(j):
        at = pl.ds(j * 2, 2)
        return pltpu.make_async_copy(gout.at[at], guesses.at[at], osem.at[j])

    def guess(j, carry):
        for k in range(2):
            g = g_in[pl.ds(pl.multiple_of((j * 2 + k) * 16, 16), S), :]
            lanes = slice(k * LN, (k + 1) * LN)
            comb[2 * S * k : 2 * S * k + S, lanes] = jnp.where(low12, g, -g)
            comb[2 * S * k + S : 2 * S * (k + 1), lanes] = pltpu.roll(g, NB, 1)
        vectors = bbuf[pl.ds(j * 2, 2)].reshape(2 * LN, BV)
        out = jnp.dot(comb[...].astype(BF16), vectors, preferred_element_type=F32)
        gout[j * 2] = out[0 : 2 * S]
        gout[j * 2 + 1] = out[2 * S : 4 * S]
        out_copy(j).start()
        return carry

    comb[...] = jnp.zeros_like(comb)
    lax.fori_loop(0, BLK // 2, guess, 0, unroll=8)
    for j in range(BLK // 2):
        out_copy(j).wait()


def shards(basis, sources, old_coeffs, eigenvalues, dest_owner, new_pos):
    hbm = pl.BlockSpec(memory_space=pl.ANY)
    vmem = pl.BlockSpec(memory_space=pltpu.VMEM)
    half_lanes = GROUPS * MP // 2
    g, corr, vectors = pl.pallas_call(
        kernel,
        out_shape=(
            pltpu.VMEM((BLK * 16, LN), F32),
            pltpu.VMEM((2 * S, MODES), F32),
            pltpu.VMEM((BLK, LN, BV), BF16),
        ),
        in_specs=[hbm] * 7,
        out_specs=(vmem, vmem, vmem),
        scratch_shapes=[
            pltpu.VMEM((1, RECS), I32),
            pltpu.VMEM((1, RECS), I32),
            pltpu.SMEM((RECS,), I32),
            pltpu.VMEM((1, MODES), F32),
            pltpu.VMEM((BLK, 2 * S, BV), BF16),
            pltpu.VMEM((4 * S, 2 * LN), F32),
            pltpu.VMEM((BLK * 16, LN), F32),
            pltpu.VMEM((2 * S, LN), F32),
            pltpu.VMEM((PARTS, SAME, PW), BF16),
            pltpu.VMEM((2, 8, RECS), I32),
            pltpu.VMEM((RECS // 4, LN), F32),
            pltpu.VMEM((8, GROUPS * MP), F32),
            pltpu.VMEM((RECS // 4 * RR, LN), F32),
            pltpu.VMEM((RECS, MG * LN), BF16),
            pltpu.VMEM((LN, RECS), F32),
            pltpu.VMEM((RECS, LN), F32),
            pltpu.VMEM((3, 2 * RECS, SAME), BF16),
            pltpu.VMEM((3, SAME, 2 * RECS), BF16),
            pltpu.VMEM((RECS * MP, LN), F32),
            pltpu.VMEM((RECS * MP, LN), BF16),
            pltpu.VMEM((PARTS, RECS, PW), BF16),
            pltpu.VMEM((PARTS, RECS, PW), BF16),
            pltpu.VMEM((PARTS, RECS, PW), BF16),
            pltpu.VMEM((RECS * RR, LN), F32),
            pltpu.VMEM((H, RR, GROUPS * MP), F32),
            pltpu.VMEM((H, 2, 8, 8, half_lanes), F32),
            pltpu.VMEM((H, 2, 4, 8, half_lanes), F32),
            pltpu.VMEM((H, 2, 2, 4, 8, half_lanes), F32),
            pltpu.VMEM((2 * S, GROUPS * MP), F32),
            pltpu.VMEM((H, GROUPS, RR, LN), BF16),
            pltpu.VMEM((RECS * 8, LN), F32),
            pltpu.VMEM((H, 2 * RECS, HW), BF16),
            pltpu.VMEM((PARTS, PLANE, PW), BF16),
            pltpu.VMEM((PARTS, 2, 2, LINE, PW), BF16),
            pltpu.VMEM((PARTS, 2, PLANE, PW), F32),
            pltpu.VMEM((PARTS, 2, PLANE, PW), BF16),
            pltpu.VMEM((PARTS, 2, 4, LINE, PW), BF16),
            pltpu.VMEM((PARTS, PLANE, PW), F32),
            pltpu.VMEM((PARTS, 3, LINE, PW), BF16),
            pltpu.VMEM((PARTS, 3, LINE, PW), BF16),
            pltpu.VMEM((PARTS, 3, BLK, PW), BF16),
            pltpu.VMEM((PARTS, 3, BLK, PW), BF16),
            pltpu.VMEM((BLK * 16, LN), F32),
            pltpu.SemaphoreType.DMA((BLK // 2,)),
            pltpu.SemaphoreType.DMA((BLK // 2,)),
            pltpu.SemaphoreType.DMA,
            pltpu.SemaphoreType.DMA((4,)),
            pltpu.SemaphoreType.DMA((N_COPIES,)),
            pltpu.SemaphoreType.DMA((N_COPIES,)),
        ],
        compiler_params=pltpu.CompilerParams(
            collective_id=1, has_side_effects=True, vmem_limit_bytes=46 * MIB
        ),
    )(
        basis, sources, old_coeffs, dest_owner.reshape(1, RECS), new_pos.reshape(1, RECS),
        new_pos, eigenvalues.reshape(1, MODES),
    )
    guesses, correlations = pl.pallas_call(
        guess_kernel,
        out_shape=(
            jax.ShapeDtypeStruct((BLK, 2 * S, BV), F32),
            jax.ShapeDtypeStruct((2 * S, MODES), F32),
        ),
        in_specs=[vmem, vmem, vmem],
        out_specs=(hbm, vmem),
        scratch_shapes=[
            pltpu.VMEM((4 * S, 2 * LN), F32),
            pltpu.VMEM((BLK, 2 * S, BV), F32),
            pltpu.SemaphoreType.DMA((BLK // 2,)),
        ],
        compiler_params=pltpu.CompilerParams(vmem_limit_bytes=16 * MIB),
    )(g, corr, vectors)
    return guesses, correlations.T


def solution(mesh):
    in_specs = (
        P(("gz", "ta"), None, None),
        P(("gz", "ta"), None, None),
        P(("gz", "ta"), None),
        P(),
        P(("gz", "ta")),
        P(("gz", "ta")),
    )
    out_specs = (P(("gz", "ta"), None, None), P())
    return jax.shard_map(shards, mesh=mesh, in_specs=in_specs, out_specs=out_specs, check_vma=False)
```

```python
import jax
import jax.numpy as jnp
from jax import lax
from jax.experimental import pallas as pl
from jax.experimental.pallas import tpu as pltpu
from jax.sharding import PartitionSpec as P

F32 = jnp.float32
BF16 = jnp.bfloat16
I32 = jnp.int32
MESH = pl.DeviceIdType.MESH

NB = 64
LN = 2 * NB
BV = 3072
S = 12
BLK = 16
MG = 25
MP = 32
GROUPS = 16
RECS = 256
MODES = 400
H = 2
SH = S // H
PARTS = 3 * H
PW = 2 * LN
HW = SH * LN
RR = 16
SAME = 64 * BLK
PLANE, LINE = 16 * BLK, 4 * BLK
MIB = 1 << 20
N_COPIES = 1 + PARTS * 22 + PARTS + H * (14 + 6 + 14) + 2 * H + PARTS * 18


class Place:
    def __init__(self):
        gz = lax.axis_index("gz")
        ta = lax.axis_index("ta")
        self.core = lax.rem(gz, 2)
        self.c = (ta // 4, gz // 2, lax.rem(ta, 4))
        self.known = {}

    def at(self, axis, d):
        if (axis, d) not in self.known:
            self.known[axis, d] = lax.rem(self.c[axis] + d, 4) if d else self.c[axis]
        return self.known[axis, d]

    def device(self, axis, d, flip=False):
        if (axis, d, flip) not in self.known:
            x, y, z = (self.at(a, d) if a == axis else self.c[a] for a in range(3))
            core = 1 - self.core if flip else self.core
            self.known[axis, d, flip] = (y * 2 + core, x * 4 + z)
        return self.known[axis, d, flip]


def order(q):
    return (q % 3, (q + 1) % 3, (q + 2) % 3)


class Copies:
    def __init__(self, send, recv):
        self.send, self.recv, self.all, self.settled = send, recv, [], 0

    def start(self, src, dst, device):
        n = len(self.all)
        copy = pltpu.make_async_remote_copy(
            src_ref=src,
            dst_ref=dst,
            send_sem=self.send.at[n],
            recv_sem=self.recv.at[n],
            device_id=device,
            device_id_type=MESH,
        )
        copy.start()
        self.all.append(copy)
        return copy

    def settle(self, until=None):
        until = len(self.all) if until is None else until
        for copy in self.all[self.settled : until]:
            copy.wait_send()
        self.settled = until


def arrived(copies):
    for copy in copies:
        copy.wait_recv()


def iota(shape, axis):
    return lax.broadcasted_iota(I32, shape, axis)


def low_lanes(shape):
    return iota(shape, 1) % LN < NB


def spread_lanes(x):
    x = x + pltpu.roll(x, 2 * MP, 1)
    return x + pltpu.roll(x, MP, 1)


def kernel(
    basis, sources, coeffs_in, owner_hbm, pos_hbm, pos_flat, eig_hbm,
    g_out, corr_out, bbuf,
    owner_in, pos_in, pos, eig_in, sbuf, prod, stage, sq, table, idsb, lane_group, eig, terms, coeffs, kbig, kcol, pick, pick_t, wide, modes,
    mine, theirs, got, xs, pay, ar1, ar2, ar3, corr, wt, tall, both,
    far_out, far_in, near_sum, near_out, near_in, x, line_out, line_in, own_out, own_in, gs,
    bsem, ssem, csem, isem, send, recv,
):
    place = Place()
    core = place.core
    sib = place.device(0, 0, True)
    copies = Copies(send, recv)

    def pair_load(j):
        at = pl.ds(j * 2, 2)
        return (
            pltpu.make_async_copy(sources.at[at], sbuf.at[at], ssem.at[j]),
            pltpu.make_async_copy(basis.at[at], bbuf.at[at], bsem.at[j]),
        )

    for j in range(3):
        for copy in pair_load(j):
            copy.start()
    load_coeffs = pltpu.make_async_copy(coeffs_in, coeffs, csem)
    load_coeffs.start()
    small_loads = [
        pltpu.make_async_copy(src, dst, isem.at[k])
        for k, (src, dst) in enumerate(
            ((owner_hbm, owner_in), (pos_hbm, pos_in), (pos_flat, pos), (eig_hbm, eig_in))
        )
    ]
    for copy in small_loads:
        copy.start()
    barrier = pltpu.get_barrier_semaphore()
    friends = [sib] + [place.device(a, d, f) for a in range(3) for d in (1, 2, 3) for f in (False, True)]
    for friend in friends:
        pl.semaphore_signal(barrier, inc=1, device_id=friend, device_id_type=MESH)

    low12 = low_lanes((S, LN))

    def block_pair(j, total):
        for copy in pair_load(j):
            copy.wait()

        @pl.when(j + 3 < BLK // 2)
        def _():
            for copy in pair_load(j + 3):
                copy.start()

        at = pl.ds(j * 2, 2)
        field = sbuf[at].reshape(4 * S, BV)
        vectors = bbuf[at].reshape(2 * LN, BV)
        prod[...] = lax.dot_general(
            field, vectors, (((1,), (1,)), ((), ())), preferred_element_type=F32
        )
        for k in range(2):
            lanes = slice(k * LN, (k + 1) * LN)
            a = prod[2 * S * k : 2 * S * k + S, lanes]
            b = pltpu.roll(prod[2 * S * k + S : 2 * S * k + 2 * S, lanes], NB, 1)
            stage[pl.ds(pl.multiple_of((j * 2 + k) * 16, 16), S), :] = b + jnp.where(low12, a, -a)
        wide_field = field.astype(F32)
        wide_field = wide_field * wide_field
        for t in range(BV // LN):
            total = total + wide_field[:, t * LN : (t + 1) * LN]
        return total

    total = lax.fori_loop(0, BLK // 2, block_pair, jnp.zeros((4 * S, LN), F32))
    pl.semaphore_wait(barrier, len(friends))

    def row(c3, c2, c1=0):
        return pl.multiple_of(((c3 * 4 + c2) * 4 + c1) * BLK, BLK)

    def rows(q, start, size):
        return table.at[q, pl.ds(start, size), :]

    first, second, third, last = {}, {}, {}, {}

    def to_axis(q, axis, start, size, ds):
        ref = rows(q, start, size)
        return [copies.start(ref, ref, place.device(axis, d)) for d in ds]

    def ag1(q):
        a1, a2, a3 = order(q)
        here = row(place.c[a3], place.c[a2], place.c[a1])
        s = q * 2
        own = [stage[pl.ds(s + k, BLK, stride=16), :] for k in range(2)]
        table[q, pl.ds(here, BLK), :] = jnp.concatenate(own, axis=1).astype(BF16)
        first[q] = to_axis(q, a1, here, BLK, (2, 1, 3))

    def ag2(q):
        _, a2, a3 = order(q)
        arrived(first[q])
        second[q] = to_axis(q, a2, row(place.c[a3], place.c[a2]), LINE, (1, 3, 2))

    def ag3(q, d):
        _, a2, a3 = order(q)
        if d:
            second[q][{3: 0, 1: 1, 2: 2}[d]].wait_recv()
        third[q, d] = to_axis(q, a3, row(place.c[a3], place.at(a2, d)), LINE, (1, 3))

    def ag_forward(q, d):
        _, a2, a3 = order(q)
        arrived(third[q, d])
        c2 = place.at(a2, d)
        half = LINE // 2
        a = rows(q, row(place.at(a3, 3), c2), half)
        b = rows(q, pl.multiple_of(row(place.at(a3, 1), c2) + half, BLK), half)
        last[q, d] = [
            copies.start(a, a, place.device(a3, 1)),
            copies.start(b, b, place.device(a3, 3)),
        ]

    def make_keys():
        kbig[...] = jnp.zeros_like(kbig)
        for who in range(2):
            owner, at = idsb[who, 0:1, :], idsb[who, 1:2, :]
            c = ((owner >> 2) & 3, owner >> 5, owner & 3)
            same = ((owner >> 4) & 1) == core
            for p in range(3):
                a1, a2, a3 = order(p)
                key = ((c[a3] * 4 + c[a2]) * 4 + c[a1]) * BLK + (at >> 4)
                key = jnp.where(same, key, -1)
                kbig[who * 3 + p : who * 3 + p + 1, :] = key.astype(F32)
        kcol[...] = kbig[...].T

    def make_picks():
        wide_ids = iota((RECS, SAME), 1).astype(F32)
        for who in range(2):
            for p in range(3):
                k = who * 3 + p
                pick[p, (1 - who) * RECS : (2 - who) * RECS, :] = jnp.where(kcol[:, k : k + 1] == wide_ids, 1.0, 0.0).astype(BF16)

    def make_picks_t():
        tall_ids = iota((SAME, RECS), 0).astype(F32)
        for who in range(2):
            for p in range(3):
                k = who * 3 + p
                pick_t[p, :, who * RECS : (who + 1) * RECS] = jnp.where(
                    kbig[k : k + 1, :] == tall_ids, 1.0, 0.0
                ).astype(BF16)

    def make_modes():
        for m in range(MG):
            wide[pl.ds(m, RECS, stride=MP), :] = coeffs[:, m * LN : (m + 1) * LN].astype(F32)
        for m in range(MG, MP):
            wide[pl.ds(m, RECS, stride=MP), :] = jnp.zeros((RECS, LN), F32)
        modes[...] = wide[...].astype(BF16)

    def make_tables():
        i = iota((RECS // 4, RECS), 1)
        group = jnp.where(i // 4 == iota((RECS // 4, RECS), 0), pos_in[...] & (GROUPS - 1), 0)
        lanes = iota((RECS, LN), 0) % 4 == iota((RECS, LN), 1) // MP
        lane_group[...] = jnp.dot(
            group.astype(F32).astype(BF16),
            jnp.where(lanes, 1.0, 0.0).astype(BF16),
            preferred_element_type=F32,
        )
        wide_eig = jnp.concatenate([eig_in[...], jnp.ones((1, GROUPS * MP - MODES), F32)], axis=1)
        lane = iota((1, GROUPS * MP), 1)
        padded = jnp.full((1, GROUPS * MP), jnp.inf, F32)
        for r in range(GROUPS):
            moved = pltpu.roll(wide_eig, r * (MP - MG), 1) if r else wide_eig
            padded = jnp.where((lane // MP == r) & (lane % MP < MG), moved, padded)
        eig[...] = jnp.broadcast_to(padded, eig.shape)

    exchange = {}

    def gather(h):
        for p in range(3):
            q = h * 3 + p
            for d in range(4):
                arrived(last[q, d])
            found = jnp.dot(pick[p, 0:RECS], table[q], preferred_element_type=F32)
            theirs[q] = found.astype(BF16)
            exchange[q] = copies.start(theirs.at[q], got.at[q], sib)
        for p in range(3):
            q = h * 3 + p
            found = jnp.dot(pick[p, RECS : 2 * RECS], table[q], preferred_element_type=F32)
            mine[q] = found.astype(BF16)

    low_rec = low_lanes((RECS, LN))
    group32 = iota((RR, LN), 1) // MP

    def project_start(h):
        for p in range(3):
            q = h * 3 + p
            exchange[q].wait_recv()
            both_cores = mine[q].astype(F32) + got[q].astype(F32)
            for k in range(2):
                real = both_cores[:, k * LN : (k + 1) * LN]
                turned = pltpu.roll(real, NB, 1)
                xs[pl.ds(2 * p + k, RECS, stride=RR), :] = real
                xs[pl.ds(8 + 2 * p + k, RECS, stride=RR), :] = jnp.where(low_rec, turned, -turned)

    def project(h):
        def eight(g, carry):
            left = xs[pl.ds(pl.multiple_of(g * 8 * RR, 8 * RR), 8 * RR), :].astype(BF16)
            right = modes[pl.ds(pl.multiple_of(g * 8 * MP, 8 * MP), 8 * MP), :]
            out = lax.dot_general(left, right, (((1,), (1,)), ((), ())), preferred_element_type=F32)
            for t in range(2):
                lanes = slice(t * LN, (t + 1) * LN)
                term = out[4 * t * RR : (4 * t + 1) * RR, lanes]
                for k in range(1, 4):
                    a = 4 * t + k
                    term = jnp.where(group32 == k, out[a * RR : (a + 1) * RR, lanes], term)
                terms[pl.ds(pl.multiple_of((g * 2 + t) * RR, RR), RR), :] = term
            return carry

        lax.fori_loop(0, RECS // 8, eight, 0, unroll=8)

        def four(g, acc):
            term = terms[pl.ds(pl.multiple_of(g * RR, RR), RR), :]
            whose = lane_group[pl.ds(g, 1), :]
            return tuple(acc[r] + jnp.where(whose == float(r), term, 0.0) for r in range(GROUPS))

        acc = lax.fori_loop(0, RECS // 4, four, (jnp.zeros((RR, LN), F32),) * GROUPS, unroll=4)
        for t in range(4):
            tile = spread_lanes(acc[4 * t])
            for k in range(1, 4):
                tile = jnp.where(group32 == k, spread_lanes(acc[4 * t + k]), tile)
            pay[h, :, t * LN : (t + 1) * LN] = tile
        norm = sq[h * SH : (h + 1) * SH, :] + sq[S + h * SH : S + (h + 1) * SH, :]
        lane = iota((SH, LN), 1)
        for base in (0, 8):
            old = pay[h, base : base + SH, 0:LN]
            pay[h, base : base + SH, 0:LN] = jnp.where(lane == MG, norm, old)

    steps = {}
    half_lanes = GROUPS * MP // 2

    def axis_of(h, v, step):
        return (v + h + step) % 3

    def sum1(h):
        for v in range(2):
            axis = axis_of(h, v, 0)
            slot = place.c[axis] * 2 + core
            piece = slice(8 * v, 8 * v + 8)
            ours = pl.ds(pl.multiple_of(core * half_lanes, half_lanes), half_lanes)
            other = pl.ds(pl.multiple_of((1 - core) * half_lanes, half_lanes), half_lanes)
            ar1[h, v, slot] = pay[h, piece, ours]
            dst = ar1.at[h, v, slot]
            steps[1, h, v] = [
                copies.start(pay.at[h, piece, other if f else ours], dst, place.device(axis, d, f))
                for d in (2, 1, 3, 0) for f in (False, True) if d or f
            ]

    def sum2(h):
        for v in range(2):
            arrived(steps[1, h, v])
            total = ar1[h, v, 0]
            for k in range(1, 8):
                total = total + ar1[h, v, k]
            axis = axis_of(h, v, 1)
            slot = place.c[axis]
            ar2[h, v, slot] = total
            ref = ar2.at[h, v, slot]
            steps[2, h, v] = [copies.start(ref, ref, place.device(axis, d)) for d in (2, 1, 3)]

    def sum3(h):
        for v in range(2):
            arrived(steps[2, h, v])
            total = (ar2[h, v, 0] + ar2[h, v, 1]) + (ar2[h, v, 2] + ar2[h, v, 3])
            axis = axis_of(h, v, 2)
            slot = place.c[axis]
            ar3[h, v, core, slot] = total
            ref = ar3.at[h, v, core, slot]
            steps[3, h, v] = [
                copies.start(ref, ref, place.device(axis, d, f))
                for d in (2, 1, 3, 0) for f in (False, True) if d or f
            ]

    def weigh(h):
        for v in range(2):
            arrived(steps[3, h, v])
        scale = None
        for t in range(4):
            k, lanes = t // 2, slice((t % 2) * LN, (t % 2 + 1) * LN)
            tile = jnp.concatenate(
                [
                    (ar3[h, v, k, 0, :, lanes] + ar3[h, v, k, 1, :, lanes])
                    + (ar3[h, v, k, 2, :, lanes] + ar3[h, v, k, 3, :, lanes])
                    for v in range(2)
                ],
                axis=0,
            )
            if scale is None:
                norm_sq = tile[:, MG : MG + 1]
                cells = jnp.float32(2 * 128 * BLK * BV)
                scale = jnp.sqrt(cells) * lax.rsqrt(norm_sq + 1e-06)
            tile = tile * scale
            corr[h * SH : (h + 1) * SH, t * LN : (t + 1) * LN] = tile[0:SH]
            corr[S + h * SH : S + (h + 1) * SH, t * LN : (t + 1) * LN] = tile[8 : 8 + SH]
            weights = tile / eig[0:1, t * LN : (t + 1) * LN]
            for k in range(4):
                wt[h, 4 * t + k] = spread_lanes(jnp.where(group32 == k, weights, 0.0)).astype(BF16)

    def mix(h):
        low8 = low_lanes((8, LN))
        zero = jnp.zeros((RR, LN), BF16)

        def eight(g, carry):
            strips = []
            for a in range(8):
                group = pos[g * 8 + a] & (GROUPS - 1)
                strip = jnp.where(group32 == a % 4, wt[h, group], zero)
                pair = [strip, zero] if a < 4 else [zero, strip]
                strips.append(jnp.concatenate(pair, axis=1))
            left = jnp.concatenate(strips, axis=0)
            right = modes[pl.ds(pl.multiple_of(g * 8 * MP, 8 * MP), 8 * MP), :]
            out = jnp.dot(left, right, preferred_element_type=F32)
            for a in range(8):
                real, imag = out[a * RR : a * RR + 8], out[a * RR + 8 : a * RR + 16]
                turned = pltpu.roll(imag, NB, 1)
                at = pl.ds(pl.multiple_of((g * 8 + a) * 8, 8), 8)
                tall[at, :] = real + jnp.where(low8, -turned, turned)
            return carry

        half = RECS // 2
        exchange["g", h] = []
        for k in range(2):
            lax.fori_loop(k * half // 8, (k + 1) * half // 8, eight, 0, unroll=8)
            ours = slice(k * half, (k + 1) * half)
            for s in range(SH):
                part = tall[pl.ds(k * half * 8 + s, half, stride=8), :]
                both[h, ours, s * LN : (s + 1) * LN] = part.astype(BF16)
            away = both.at[h, RECS + k * half : RECS + (k + 1) * half]
            exchange["g", h].append(copies.start(both.at[h, ours], away, sib))

    def partial(q, c3):
        h, p = q // 3, q % 3
        at = pl.ds(pl.multiple_of(c3 * PLANE, PLANE), PLANE)
        return jnp.dot(
            pick_t[p, at, :], both[h, :, p * PW : (p + 1) * PW], preferred_element_type=F32
        )

    far, near, lines, owns = {}, {}, {}, {}

    by_side = ((2, 1), (3, 0))

    def line_at(axis, d, size):
        return pl.ds(pl.multiple_of(place.at(axis, d) * size, size), size)

    def rs1(q):
        _, a2, a3 = order(q)
        far_out[q] = partial(q, place.at(a3, 2)).astype(BF16)
        for k, d in enumerate((1, 3)):
            for j, n in enumerate(by_side[k]):
                far[q, k, j] = copies.start(
                    far_out.at[q, line_at(a2, n, LINE), :], far_in.at[q, k, j], place.device(a3, d)
                )

    def send_near(q, k, n):
        _, a2, a3 = order(q)
        near[q, k, n] = copies.start(
            near_out.at[q, k, line_at(a2, n, LINE), :],
            near_in.at[q, k, n],
            place.device(a3, (1, 3)[k]),
        )

    def rs_near(q):
        _, a2, a3 = order(q)
        for k, d in enumerate((1, 3)):
            near_sum[q, k] = partial(q, place.at(a3, d))
            for n in by_side[1 - k]:
                at = line_at(a2, n, LINE)
                near_out[q, k, at, :] = near_sum[q, k, at, :].astype(BF16)
                send_near(q, k, n)

    def rs2(q):
        a2 = order(q)[1]
        for k in range(2):
            for j, n in enumerate(by_side[k]):
                far[q, k, j].wait_recv()
                at = line_at(a2, n, LINE)
                total = near_sum[q, k, at, :] + far_in[q, k, j].astype(F32)
                near_out[q, k, at, :] = total.astype(BF16)
                send_near(q, k, n)

    def rs_own(q):
        x[q] = partial(q, place.c[order(q)[2]])

    def whole_line(q, n):
        total = x[q, line_at(order(q)[1], n, LINE), :]
        for k in range(2):
            near[q, k, n].wait_recv()
            total = total + near_in[q, k, n].astype(F32)
        return total

    def rs3(q):
        a2 = order(q)[1]
        for n in (2, 1, 3):
            line_out[q, n - 1] = whole_line(q, n).astype(BF16)
            lines[q, n] = copies.start(
                line_out.at[q, n - 1], line_in.at[q, n - 1], place.device(a2, n)
            )

    def rs4(q):
        a1 = order(q)[0]
        total = whole_line(q, 0)
        for n in (1, 3, 2):
            lines[q, n].wait_recv()
            total = total + line_in[q, n - 1].astype(F32)
        x[q, 0:LINE, :] = total
        owns[q] = []
        for k, d in enumerate((2, 1, 3)):
            own_out[q, k] = x[q, line_at(a1, d, BLK), :].astype(BF16)
            owns[q].append(copies.start(own_out.at[q, k], own_in.at[q, k], place.device(a1, d)))

    def rs5(q):
        total = x[q, line_at(order(q)[0], 0, BLK), :]
        for k in range(3):
            owns[q][k].wait_recv()
            total = total + own_in[q, k].astype(F32)
        for k in range(2):
            gs[pl.ds(q * 2 + k, BLK, stride=16), :] = total[:, k * LN : (k + 1) * LN]

    h0, h1 = (0, 1, 2), (3, 4, 5)
    for q in h0 + h1:
        ag1(q)
    sq[...] = jnp.broadcast_to(
        jnp.sum(total[0 : 2 * S] + total[2 * S : 4 * S], axis=1, keepdims=True), (2 * S, LN)
    )
    for copy in small_loads:
        copy.wait()
    idsb[0] = jnp.zeros((8, RECS), I32)
    idsb[0, 0:1, :] = owner_in[...]
    idsb[0, 1:2, :] = pos_in[...]
    id_copy = copies.start(idsb.at[0], idsb.at[1], sib)
    load_coeffs.wait()
    make_modes()
    make_tables()
    for s in (6, 7, 14, 15):
        xs[pl.ds(s, RECS, stride=RR), :] = jnp.zeros((RECS, LN), F32)
    for hq in (h0, h1):
        for q in hq:
            ag2(q)
        for q in hq:
            ag3(q, 0)
    id_copy.wait_recv()
    make_keys()
    make_picks()
    for hq in (h0, h1):
        for d in (3, 1, 2):
            for q in hq:
                ag3(q, d)
    make_picks_t()
    for d in (0, 3, 1, 2):
        for q in h0:
            ag_forward(q, d)
    for d in (0, 3, 1, 2):
        for q in h1:
            ag_forward(q, d)
    gather(0)
    project_start(0)
    project(0)
    sum1(0)
    gather(1)
    project_start(1)
    sum2(0)
    project(1)
    sum1(1)
    sum3(0)
    sum2(1)
    weigh(0)
    mix(0)
    sum3(1)
    arrived(exchange["g", 0])
    for q in h0:
        rs1(q)
    for q in h0:
        rs_near(q)
    weigh(1)
    mix(1)
    for q in h0:
        rs2(q)
    arrived(exchange["g", 1])
    for q in h1:
        rs1(q)
    for q in h1:
        rs_near(q)
    for q in h0 + h1:
        rs_own(q)
    for q in h0:
        rs3(q)
    far_sent = len(copies.all)
    for q in h1:
        rs2(q)
    copies.settle(far_sent)
    for r in range(GROUPS):
        corr_out[:, r * MG : (r + 1) * MG] = corr[:, r * MP : r * MP + MG]
    for q in h1:
        rs3(q)
    for q in h0:
        rs4(q)
    copies.settle()
    for q in h1:
        rs4(q)
    for q in h0 + h1:
        rs5(q)
    g_out[...] = gs[...]
    copies.settle()


def guess_kernel(g_in, corr_in, bbuf, guesses, corr_out, comb, gout, osem):
    corr_out[...] = corr_in[...]
    low12 = low_lanes((S, LN))

    def out_copy(j):
        at = pl.ds(j * 2, 2)
        return pltpu.make_async_copy(gout.at[at], guesses.at[at], osem.at[j])

    def guess(j, carry):
        for k in range(2):
            g = g_in[pl.ds(pl.multiple_of((j * 2 + k) * 16, 16), S), :]
            lanes = slice(k * LN, (k + 1) * LN)
            comb[2 * S * k : 2 * S * k + S, lanes] = jnp.where(low12, g, -g)
            comb[2 * S * k + S : 2 * S * (k + 1), lanes] = pltpu.roll(g, NB, 1)
        vectors = bbuf[pl.ds(j * 2, 2)].reshape(2 * LN, BV)
        out = jnp.dot(comb[...].astype(BF16), vectors, preferred_element_type=F32)
        gout[j * 2] = out[0 : 2 * S]
        gout[j * 2 + 1] = out[2 * S : 4 * S]
        out_copy(j).start()
        return carry

    comb[...] = jnp.zeros_like(comb)
    lax.fori_loop(0, BLK // 2, guess, 0, unroll=8)
    for j in range(BLK // 2):
        out_copy(j).wait()


def shards(basis, sources, old_coeffs, eigenvalues, dest_owner, new_pos):
    hbm = pl.BlockSpec(memory_space=pl.ANY)
    vmem = pl.BlockSpec(memory_space=pltpu.VMEM)
    half_lanes = GROUPS * MP // 2
    g, corr, vectors = pl.pallas_call(
        kernel,
        out_shape=(
            pltpu.VMEM((BLK * 16, LN), F32),
            pltpu.VMEM((2 * S, MODES), F32),
            pltpu.VMEM((BLK, LN, BV), BF16),
        ),
        in_specs=[hbm] * 7,
        out_specs=(vmem, vmem, vmem),
        scratch_shapes=[
            pltpu.VMEM((1, RECS), I32),
            pltpu.VMEM((1, RECS), I32),
            pltpu.SMEM((RECS,), I32),
            pltpu.VMEM((1, MODES), F32),
            pltpu.VMEM((BLK, 2 * S, BV), BF16),
            pltpu.VMEM((4 * S, 2 * LN), F32),
            pltpu.VMEM((BLK * 16, LN), F32),
            pltpu.VMEM((2 * S, LN), F32),
            pltpu.VMEM((PARTS, SAME, PW), BF16),
            pltpu.VMEM((2, 8, RECS), I32),
            pltpu.VMEM((RECS // 4, LN), F32),
            pltpu.VMEM((8, GROUPS * MP), F32),
            pltpu.VMEM((RECS // 4 * RR, LN), F32),
            pltpu.VMEM((RECS, MG * LN), BF16),
            pltpu.VMEM((LN, RECS), F32),
            pltpu.VMEM((RECS, LN), F32),
            pltpu.VMEM((3, 2 * RECS, SAME), BF16),
            pltpu.VMEM((3, SAME, 2 * RECS), BF16),
            pltpu.VMEM((RECS * MP, LN), F32),
            pltpu.VMEM((RECS * MP, LN), BF16),
            pltpu.VMEM((PARTS, RECS, PW), BF16),
            pltpu.VMEM((PARTS, RECS, PW), BF16),
            pltpu.VMEM((PARTS, RECS, PW), BF16),
            pltpu.VMEM((RECS * RR, LN), F32),
            pltpu.VMEM((H, RR, GROUPS * MP), F32),
            pltpu.VMEM((H, 2, 8, 8, half_lanes), F32),
            pltpu.VMEM((H, 2, 4, 8, half_lanes), F32),
            pltpu.VMEM((H, 2, 2, 4, 8, half_lanes), F32),
            pltpu.VMEM((2 * S, GROUPS * MP), F32),
            pltpu.VMEM((H, GROUPS, RR, LN), BF16),
            pltpu.VMEM((RECS * 8, LN), F32),
            pltpu.VMEM((H, 2 * RECS, HW), BF16),
            pltpu.VMEM((PARTS, PLANE, PW), BF16),
            pltpu.VMEM((PARTS, 2, 2, LINE, PW), BF16),
            pltpu.VMEM((PARTS, 2, PLANE, PW), F32),
            pltpu.VMEM((PARTS, 2, PLANE, PW), BF16),
            pltpu.VMEM((PARTS, 2, 4, LINE, PW), BF16),
            pltpu.VMEM((PARTS, PLANE, PW), F32),
            pltpu.VMEM((PARTS, 3, LINE, PW), BF16),
            pltpu.VMEM((PARTS, 3, LINE, PW), BF16),
            pltpu.VMEM((PARTS, 3, BLK, PW), BF16),
            pltpu.VMEM((PARTS, 3, BLK, PW), BF16),
            pltpu.VMEM((BLK * 16, LN), F32),
            pltpu.SemaphoreType.DMA((BLK // 2,)),
            pltpu.SemaphoreType.DMA((BLK // 2,)),
            pltpu.SemaphoreType.DMA,
            pltpu.SemaphoreType.DMA((4,)),
            pltpu.SemaphoreType.DMA((N_COPIES,)),
            pltpu.SemaphoreType.DMA((N_COPIES,)),
        ],
        compiler_params=pltpu.CompilerParams(
            collective_id=1, has_side_effects=True, vmem_limit_bytes=46 * MIB
        ),
    )(
        basis, sources, old_coeffs, dest_owner.reshape(1, RECS), new_pos.reshape(1, RECS),
        new_pos, eigenvalues.reshape(1, MODES),
    )
    guesses, correlations = pl.pallas_call(
        guess_kernel,
        out_shape=(
            jax.ShapeDtypeStruct((BLK, 2 * S, BV), F32),
            jax.ShapeDtypeStruct((2 * S, MODES), F32),
        ),
        in_specs=[vmem, vmem, vmem],
        out_specs=(hbm, vmem),
        scratch_shapes=[
            pltpu.VMEM((4 * S, 2 * LN), F32),
            pltpu.VMEM((BLK, 2 * S, BV), F32),
            pltpu.SemaphoreType.DMA((BLK // 2,)),
        ],
        compiler_params=pltpu.CompilerParams(vmem_limit_bytes=16 * MIB),
    )(g, corr, vectors)
    return guesses, correlations.T


def solution(mesh):
    in_specs = (
        P(("gz", "ta"), None, None),
        P(("gz", "ta"), None, None),
        P(("gz", "ta"), None),
        P(),
        P(("gz", "ta")),
        P(("gz", "ta")),
    )
    out_specs = (P(("gz", "ta"), None, None), P())
    return jax.shard_map(shards, mesh=mesh, in_specs=in_specs, out_specs=out_specs, check_vma=False)
```
